32 devices in a mesh: grp: 4 (over x, core), hub: 8 (over z, y).
Axes of the slice: x: 2, y: 2, z: 4, core: 2. Of those that a mesh axis runs over, the one named last changes fastest.
Arguments:
- embed: bfloat16 [262144, 128], P(('grp', 'hub')), may hold values from -6 to 6
- hub_ids: int32 [32, 4], P(('grp', 'hub')), may hold values from 0 to 63
- send_ids: int32 [32, 4, 4], P(('grp', 'hub')), may hold values from 0 to 63
- tile_row: int32 [32, 192], P(('grp', 'hub')), may hold values from 0 to 63
- tile_col: int32 [32, 192], P(('grp', 'hub')), may hold values from 0 to 111
- tile_val: bfloat16 [6144, 128, 128], P(('grp', 'hub')), may hold values from -0.3125 to 0.3125
- tile_count: int32 [32], P(('grp', 'hub')), may hold values from 96 to 192, as said below
Outputs:
- spectral: float32 [262144, 128], P(('grp', 'hub'))
The draws below stay inside these ranges and needn't reach their ends.
Inputs may be any that keep to these rules, and one draw needn't show every extreme that they name: `tile_count`: each device has at least 96 live tile slots and some device has all 192 live; slots at or past a device's count are ignored.
All inputs are finite; a program needn't handle non-finite values.
Results may differ from the reference program's by a relative error of at most 0.0051.
Values may be sent and summed in bfloat16 or wider, within the bound.
No kernel may reach another device: no remote copies, remote signals or barrier semaphores. Data moves between devices by JAX's collectives and lax.ppermute only.
A program may use at most 128 MiB of HBM per device.

```python
import math
import jax
import jax.numpy as jnp
import numpy as np
from jax import lax

EMB = 128
BLK = 128
NB_DEV = 64
TILES = 192
HUB_DEV = 4
TAIL_K = 4
ORDER = 4
NODES = 262144
COLS = 112
N_GRP = 4
N_HUB = 8
DEVICES = 32


def draw_tile_count(key, part):
    counts = jax.random.randint(key, (DEVICES,), TILES // 2, TILES + 1, dtype=jnp.int32)
    position = jax.random.randint(jax.random.fold_in(key, 7), (), 0, DEVICES, dtype=jnp.int32)
    return jnp.where(jnp.arange(DEVICES, dtype=jnp.int32) == position, TILES, counts).astype(jnp.int32)


def touch_ends(entries, own_key, smallest, top_value):
    spot = [jax.random.randint(jax.random.fold_in(own_key, axis), (), 0, length) for axis, length in enumerate(entries.shape)]
    widest = entries.shape.index(max(entries.shape))
    neighbour = spot[:widest] + [(spot[widest] + 1) % entries.shape[widest]] + spot[widest + 1:]
    return entries.at[tuple(spot)].set(smallest).at[tuple(neighbour)].set(top_value)


def block_levels(own_key, extent, cuts, smallest, top_value):
    level = 1.0
    for axis_at, parts in cuts:
        draws = jax.random.uniform(jax.random.fold_in(jax.random.fold_in(own_key, 6), axis_at), (parts,), jnp.float32, smallest / len(cuts), top_value / len(cuts))
        level = level * jnp.repeat(jnp.exp(draws), extent[axis_at] // parts).reshape((-1,) + (1,) * (len(extent) - 1 - axis_at))
    return level


def rank_table(number_of, lean):
    weights = [(1 << 20) // math.isqrt(rank ** lean) + 1 for rank in range(1, number_of + 1)]
    spread = 1 + sum(weights) // (1 << 30)
    return np.cumsum(np.array([max(1, weight // spread) for weight in weights]))


def ranked(stream_key, shape, count, lean):
    grid = rank_table(count, lean)
    ticket = jax.random.randint(jax.random.fold_in(stream_key, 1), shape, 0, int(grid[count - 1]))
    grade = jnp.searchsorted(jnp.asarray(grid, jnp.int32), ticket, side="right")
    return jax.random.permutation(jax.random.fold_in(stream_key, 2), count)[grade].astype(jnp.int32)


def normal_values(rng, shape, spread, reach, split=(), kind=jnp.bfloat16):
    entries = jax.random.normal(rng, shape, jnp.float32) * spread
    if len(split) > 0:
        entries = block_levels(rng, shape, split, -0.22, 0.18) * entries
    return jnp.clip(entries, min=-reach, max=reach).astype(kind)


def setup_inputs(seed: int = 0) -> dict:
    streams_of = jax.random.split(jax.random.key(seed), 8)
    embed = normal_values(streams_of[0], (NODES, EMB), 1.0, 6.0, ((0, 32),))
    hub_ids = touch_ends(jax.random.randint(streams_of[1], (DEVICES, HUB_DEV), 0, NB_DEV), jax.random.fold_in(streams_of[1], 1), 0, NB_DEV - 1).astype(jnp.int32)
    send_ids = touch_ends(jax.random.randint(streams_of[2], (DEVICES, N_GRP, TAIL_K), 0, NB_DEV), jax.random.fold_in(streams_of[2], 1), 0, NB_DEV - 1).astype(jnp.int32)
    tile_row = touch_ends(jax.random.randint(streams_of[3], (DEVICES, TILES), 0, NB_DEV), jax.random.fold_in(streams_of[3], 1), 0, NB_DEV - 1).astype(jnp.int32)
    tile_col = touch_ends(ranked(streams_of[4], (DEVICES, TILES), COLS, 2), jax.random.fold_in(streams_of[4], 3), 0, COLS - 1).astype(jnp.int32)
    tile_val = normal_values(streams_of[5], (DEVICES * TILES, BLK, BLK), (BLK * TILES // NB_DEV) ** -0.5, 0.3125, ((0, 32),))
    tile_count = draw_tile_count(jax.random.fold_in(streams_of[7], 71), 0)
    return dict(embed=embed, hub_ids=hub_ids, send_ids=send_ids, tile_row=tile_row, tile_col=tile_col, tile_val=tile_val, tile_count=tile_count)


SHIFT = 0.2
THETA = 3.0


def bessel_scaled(order_index):
    total = 0.0
    for term in range(40):
        total += (THETA / 2.0) ** (2 * term + order_index) / (math.factorial(term) * math.factorial(term + order_index))
    return math.exp(-THETA) * total


def coefficients():
    values = [bessel_scaled(0)]
    for order_index in range(1, ORDER + 1):
        values.append(2.0 * ((-1.0) ** order_index) * bessel_scaled(order_index))
    return values


def reference(embed, hub_ids, send_ids, tile_row, tile_col, tile_val, tile_count):
    tiles = tile_val.reshape(DEVICES, TILES, BLK, BLK)
    block_range = jnp.arange(NB_DEV, dtype=jnp.int32)
    slot_range = jnp.arange(TILES, dtype=jnp.int32)

    def apply(field):
        blocks = field.reshape(DEVICES * NB_DEV, BLK, EMB)
        owned = field.reshape(DEVICES, NB_DEV * BLK, EMB)

        def one_device(device):
            group = device // N_HUB
            column = device % N_HUB
            peers = group * N_HUB + jnp.arange(N_HUB, dtype=jnp.int32)
            hub_glob = (peers[:, None] * NB_DEV + hub_ids[peers]).reshape(-1)
            owners = jnp.arange(N_GRP, dtype=jnp.int32) * N_HUB + column
            tail_glob = (owners[:, None] * NB_DEV + send_ids[owners, group]).reshape(-1)
            local_glob = device * NB_DEV + block_range
            glob = jnp.concatenate([local_glob, hub_glob, tail_glob]).astype(jnp.int32)
            space = blocks[glob]
            picked = space[tile_col[device]]
            prod = jnp.einsum("tij,tjk->tik", tiles[device].astype(jnp.float32), picked.astype(jnp.float32), precision=lax.Precision.HIGHEST)
            live = (slot_range < tile_count[device]).astype(jnp.float32)
            masked = prod * live[:, None, None]
            summed = jax.ops.segment_sum(masked, tile_row[device], num_segments=NB_DEV)
            return summed.reshape(NB_DEV * BLK, EMB) - SHIFT * owned[device].astype(jnp.float32)

        return lax.map(one_device, jnp.arange(DEVICES, dtype=jnp.int32)).reshape(NODES, EMB)

    weights = coefficients()
    previous = embed
    spectral = weights[0] * previous.astype(jnp.float32)
    current = apply(previous).astype(jnp.bfloat16)
    spectral = spectral + weights[1] * current.astype(jnp.float32)
    for order_index in range(2, ORDER + 1):
        following = (2.0 * apply(current) - previous.astype(jnp.float32)).astype(jnp.bfloat16)
        spectral = spectral + weights[order_index] * following.astype(jnp.float32)
        previous, current = current, following
    return spectral
```

```python
import functools
import math

import jax
import jax.numpy as jnp
from jax import lax
from jax.experimental import pallas as pl
from jax.experimental.pallas import tpu as pltpu
from jax.sharding import PartitionSpec as P

ORDER = 4
SHIFT = 0.2
THETA = 3.0

UNROLL = 8
BITS = 10
MASK = (1 << BITS) - 1
F32 = jnp.float32
BF16 = jnp.bfloat16


def bessel_scaled(order_index):
    total = 0.0
    for term in range(40):
        total += (THETA / 2.0) ** (2 * term + order_index) / (
            math.factorial(term) * math.factorial(term + order_index)
        )
    return math.exp(-THETA) * total


def coefficients():
    values = [bessel_scaled(0)]
    for order_index in range(1, ORDER + 1):
        values.append(2.0 * (-1.0) ** order_index * bessel_scaled(order_index))
    return values


WEIGHTS = coefficients()


def ring_order(n):
    return [i for i in range(n) if i % 2 == 0] + [i for i in range(n - 1, -1, -1) if i % 2 == 1]


def ring_position(i, n):
    return jnp.where(i % 2 == 0, i // 2, n - 1 - i // 2)


def ring_send(x, n, step):
    order = ring_order(n)
    return lax.ppermute(x, "hub", [(order[p], order[(p + step) % n]) for p in range(n)])


def grp_source(g, e, n):
    return g ^ e if n & (n - 1) == 0 else (g - e) % n


def grp_target(g, e, n):
    return g ^ e if n & (n - 1) == 0 else (g + e) % n


def vmem(x):
    return pltpu.with_memory_space_constraint(x, pltpu.VMEM)


VMEM_SPEC = pl.BlockSpec(memory_space=pltpu.VMEM)
SMEM_SPEC = pl.BlockSpec(memory_space=pltpu.SMEM)
ANY_SPEC = pl.BlockSpec(memory_space=pl.ANY)
PARAMS = pltpu.CompilerParams(vmem_limit_bytes=8 * 1024 * 1024)


class Sizes:
    def __init__(self, mesh_shape, embed, hub_ids, send_ids, tile_val):
        self.n_grp, self.n_hub = mesh_shape["grp"], mesh_shape["hub"]
        self.blk, self.emb = tile_val.shape[1], embed.shape[1]
        self.nb = embed.shape[0] // self.blk
        self.slots = tile_val.shape[0]
        self.hub = hub_ids.shape[1]
        self.tail = send_ids.shape[2]
        self.half = self.hub // 2
        self.hub_slots = (self.n_hub - 1) * self.hub
        self.rem = self.hub_slots + (self.n_grp - 1) * self.tail
        self.cap = self.slots + UNROLL
        self.off_local, self.off_first, self.off_rest = 0, self.cap, 2 * self.cap
        self.off_len = 3 * self.cap
        self.list_len = 3 * self.cap + 3
        assert max(self.slots, self.nb + 1, self.nb + self.rem) <= MASK

    def block(self, n, dtype):
        return jax.ShapeDtypeStruct((n, self.blk, self.emb), dtype)

    def block_vmem(self, n, dtype):
        return pltpu.VMEM((n, self.blk, self.emb), dtype)


def gather_kernel(z, hub_ids, send_ids, field, hub_out, *rest):
    tails, sem = rest[:-1], rest[-1]
    g = lax.axis_index("grp")
    copies = []
    for j in range(z.hub):
        copies.append((field.at[hub_ids[0, j]], hub_out.at[j]))
    for e in range(1, z.n_grp):
        for k in range(z.tail):
            copies.append((field.at[send_ids[0, grp_target(g, e, z.n_grp), k]], tails[e - 1].at[k]))
    copies = [pltpu.make_async_copy(s, d, sem.at[i]) for i, (s, d) in enumerate(copies)]
    for c in copies:
        c.start()
    for c in copies:
        c.wait()


def bin_kernel(z, hub_ids, send_ids, tile_row, tile_col, tile_count, lists, colmap, sent):
    g = lax.axis_index("grp")
    mine = ring_position(lax.axis_index("hub"), z.n_hub)

    def clear(i, c):
        sent[i] = 0
        return c

    lax.fori_loop(0, z.nb, clear, 0)

    def local_cols(i, c):
        colmap[i] = i
        return c

    lax.fori_loop(0, z.nb, local_cols, 0)
    for j in range(z.hub):
        sent[hub_ids[0, j]] = 1

    def hub_cols(h, c):
        d = mine - ring_position(h, z.n_hub)
        d = jnp.where(d < 0, d + z.n_hub, d)
        for j in range(z.hub):
            colmap[z.nb + h * z.hub + j] = jnp.where(
                d == 0, hub_ids[0, j], z.nb + (d - 1) * z.hub + j
            )
        return c

    lax.fori_loop(0, z.n_hub, hub_cols, 0)
    base = z.nb + z.n_hub * z.hub
    for e in range(z.n_grp):
        src = grp_source(g, e, z.n_grp)
        dst = grp_target(g, e, z.n_grp)
        for k in range(z.tail):
            if e == 0:
                colmap[base + src * z.tail + k] = send_ids[0, g, k]
            else:
                colmap[base + src * z.tail + k] = z.nb + z.hub_slots + (e - 1) * z.tail + k
                sent[send_ids[0, dst, k]] = 1

    def place(t, counts):
        n0, n1, n2 = counts
        row = tile_row[0, t]
        spot = colmap[tile_col[0, t]]
        local = spot < z.nb
        first = jnp.logical_and(jnp.logical_not(local), sent[row] == 1)
        rest = jnp.logical_not(jnp.logical_or(local, first))
        where = jnp.where(local, z.off_local + n0, jnp.where(first, z.off_first + n1, z.off_rest + n2))
        spot = jnp.where(local, spot, spot - z.nb)
        lists[where] = t + (row << BITS) + (spot << (2 * BITS))
        return (n0 + local.astype(jnp.int32), n1 + first.astype(jnp.int32), n2 + rest.astype(jnp.int32))

    zero = jnp.int32(0)
    counts = lax.fori_loop(0, tile_count[0], place, (zero, zero, zero))
    for n, (off, length) in enumerate(zip((z.off_local, z.off_first, z.off_rest), counts)):
        for u in range(UNROLL):
            lists[off + length + u] = z.nb << BITS
        lists[z.off_len + n] = length


def accumulate(z, lists, which, vals, source, acc):
    off = (z.off_local, z.off_first, z.off_rest)[which]
    length = lists[z.off_len + which]

    def body(i, c):
        entries = [lists[off + i * UNROLL + u] for u in range(UNROLL)]
        prods = [
            jnp.dot(vals[e & MASK], source[e >> (2 * BITS)], preferred_element_type=F32)
            for e in entries
        ]
        for e, p in zip(entries, prods):
            row = (e >> BITS) & MASK
            acc[row] = acc[row] + p
        return c

    lax.fori_loop(0, (length + UNROLL - 1) // UNROLL, body, 0)


def fetch(parts, refs, rem, sems):
    copies = []
    for i, ((slot, n), ref) in enumerate(zip(parts, refs)):
        copies.append(pltpu.make_async_copy(ref, rem.at[pl.ds(slot, n)], sems.at[i]))
    for c in copies:
        c.start()
    return copies


def start_kernel(z, lists, embed, vals, acc, spec):
    def body(r, c):
        t = embed[r].astype(F32)
        acc[r] = -SHIFT * t
        spec[r] = WEIGHTS[0] * t
        return c

    lax.fori_loop(0, z.nb, body, 0)
    accumulate(z, lists, 0, vals, embed, acc)


def edge_kernel(z, parts, step, lists, hub_ids, send_ids, vals, prev, acc_in, *rest):
    n = len(parts)
    refs, rest = rest[:n], rest[n:]
    acc, hub_out = rest[0], rest[1]
    tails = rest[2 : 2 + z.n_grp - 1]
    rem, sems = rest[-2:]
    for c in fetch(parts, refs, rem, sems):
        c.wait()
    accumulate(z, lists, 1, vals, rem, acc)
    g = lax.axis_index("grp")

    def value(row):
        if step == 1:
            return acc[row].astype(BF16)
        return (2.0 * acc[row] - prev[row].astype(F32)).astype(BF16)

    for j in range(z.hub):
        hub_out[j] = value(hub_ids[0, j])
    for e in range(1, z.n_grp):
        for k in range(z.tail):
            tails[e - 1][k] = value(send_ids[0, grp_target(g, e, z.n_grp), k])


def inner_kernel(z, parts, step, lists, vals, prev, acc_in, spec_in, *rest):
    n = len(parts)
    refs, rest = rest[:n], rest[n:]
    acc, spec, field, rem, sems = rest
    for c in fetch(parts, refs, rem, sems):
        c.wait()
    accumulate(z, lists, 2, vals, rem, acc)

    def body(r, c):
        if step == 1:
            t = acc[r].astype(BF16)
        else:
            t = (2.0 * acc[r] - prev[r].astype(F32)).astype(BF16)
        field[r] = t
        t = t.astype(F32)
        acc[r] = -SHIFT * t
        spec[r] = spec[r] + WEIGHTS[step] * t
        return c

    lax.fori_loop(0, z.nb, body, 0)
    accumulate(z, lists, 0, vals, field, acc)


def last_kernel(z, parts, lists, vals, prev, acc_in, spec_in, *rest):
    n = len(parts)
    refs, rest = rest[:n], rest[n:]
    acc, out, stage, rem, sems, out_sem = rest
    for c in fetch(parts, refs, rem, sems):
        c.wait()
    accumulate(z, lists, 1, vals, rem, acc)
    accumulate(z, lists, 2, vals, rem, acc)
    chunks = 8 if z.nb % 8 == 0 else 1
    size = z.nb // chunks
    copies = []
    for q in range(chunks):

        def body(i, c):
            r = q * size + i
            t = (2.0 * acc[r] - prev[r].astype(F32)).astype(BF16).astype(F32)
            stage[r] = spec_in[r] + WEIGHTS[ORDER] * t
            return c

        lax.fori_loop(0, size, body, 0)
        part = pl.ds(q * size, size)
        copies.append(pltpu.make_async_copy(stage.at[part], out.at[part], out_sem.at[q]))
        copies[-1].start()
    for c in copies:
        c.wait()


def exchange(z, hub, tails):
    arrays, parts = [], []
    for e in range(1, z.n_grp):
        arrays.append(
            lax.ppermute(tails[e - 1], "grp", [(i, grp_target(i, e, z.n_grp)) for i in range(z.n_grp)])
        )
        parts.append((z.hub_slots + (e - 1) * z.tail, z.tail))
    up = down = hub
    for s in range(1, (z.n_hub + 1) // 2):
        up, down = ring_send(up, z.n_hub, 1), ring_send(down, z.n_hub, -1)
        arrays += [up, down]
        parts += [((s - 1) * z.hub, z.hub), ((z.n_hub - s - 1) * z.hub, z.hub)]
    if z.n_hub % 2 == 0:
        far = (z.n_hub // 2 - 1) * z.hub
        if z.half:
            arrays.append(ring_send(up[: z.half], z.n_hub, 1))
            parts.append((far, z.half))
        arrays.append(ring_send(down[z.half :], z.n_hub, -1))
        parts.append((far + z.half, z.hub - z.half))
    return arrays, tuple(parts)


def shards(mesh_shape, embed, hub_ids, send_ids, tile_row, tile_col, tile_val, tile_count):
    z = Sizes(mesh_shape, embed, hub_ids, send_ids, tile_val)
    ngt = z.n_grp - 1
    field0 = embed.reshape(z.nb, z.blk, z.emb)
    sent_shapes = [z.block(z.hub, BF16)] + [z.block(z.tail, BF16)] * ngt

    hub, *tails = pl.pallas_call(
        functools.partial(gather_kernel, z),
        out_shape=sent_shapes,
        in_specs=[SMEM_SPEC, SMEM_SPEC, ANY_SPEC],
        out_specs=[ANY_SPEC] * (1 + ngt),
        scratch_shapes=[pltpu.SemaphoreType.DMA((z.hub + ngt * z.tail,))],
        compiler_params=PARAMS,
        name="gather",
    )(hub_ids, send_ids, field0)
    arrays, parts = exchange(z, hub, tails)

    lists = pl.pallas_call(
        functools.partial(bin_kernel, z),
        out_shape=jax.ShapeDtypeStruct((z.list_len,), jnp.int32),
        in_specs=[SMEM_SPEC] * 5,
        out_specs=SMEM_SPEC,
        scratch_shapes=[
            pltpu.SMEM((z.nb + z.n_hub * z.hub + z.n_grp * z.tail,), jnp.int32),
            pltpu.SMEM((z.nb,), jnp.int32),
        ],
        compiler_params=PARAMS,
        name="binning",
    )(hub_ids, send_ids, tile_row, tile_col, tile_count)

    vals = vmem(tile_val)
    cur = vmem(field0)
    acc, spec = pl.pallas_call(
        functools.partial(start_kernel, z),
        out_shape=[z.block_vmem(z.nb + 1, F32), z.block_vmem(z.nb, F32)],
        in_specs=[SMEM_SPEC, VMEM_SPEC, VMEM_SPEC],
        out_specs=[VMEM_SPEC] * 2,
        compiler_params=PARAMS,
        name="start",
    )(lists, cur, vals)

    prev = cur
    scratch = [
        pltpu.VMEM((z.rem, z.blk, z.emb), BF16),
        pltpu.SemaphoreType.DMA((len(parts),)),
    ]
    for step in range(1, ORDER):
        acc, hub, *tails = pl.pallas_call(
            functools.partial(edge_kernel, z, parts, step),
            out_shape=[z.block_vmem(z.nb + 1, F32)] + sent_shapes,
            in_specs=[SMEM_SPEC] * 3 + [VMEM_SPEC] * 3 + [ANY_SPEC] * len(parts),
            out_specs=[VMEM_SPEC] * (2 + ngt),
            input_output_aliases={5: 0},
            scratch_shapes=scratch,
            compiler_params=PARAMS,
            name="edge",
        )(lists, hub_ids, send_ids, vals, vmem(prev), vmem(acc), *arrays)
        new_arrays, _ = exchange(z, hub, tails)
        acc, spec, new = pl.pallas_call(
            functools.partial(inner_kernel, z, parts, step),
            out_shape=[
                z.block_vmem(z.nb + 1, F32),
                z.block_vmem(z.nb, F32),
                z.block_vmem(z.nb, BF16),
            ],
            in_specs=[SMEM_SPEC] + [VMEM_SPEC] * 4 + [ANY_SPEC] * len(parts),
            out_specs=[VMEM_SPEC] * 3,
            input_output_aliases={3: 0, 4: 1},
            scratch_shapes=scratch,
            compiler_params=PARAMS,
            name="inner",
        )(lists, vals, vmem(prev), vmem(acc), vmem(spec), *arrays)
        arrays = new_arrays
        prev, cur = cur, new

    _, out = pl.pallas_call(
        functools.partial(last_kernel, z, parts),
        out_shape=[z.block_vmem(z.nb + 1, F32), z.block(z.nb, F32)],
        in_specs=[SMEM_SPEC] + [VMEM_SPEC] * 4 + [ANY_SPEC] * len(parts),
        out_specs=[VMEM_SPEC, ANY_SPEC],
        input_output_aliases={3: 0},
        scratch_shapes=[pltpu.VMEM((z.nb, z.blk, z.emb), F32)]
        + scratch
        + [pltpu.SemaphoreType.DMA((8,))],
        compiler_params=PARAMS,
        name="last",
    )(lists, vals, vmem(prev), vmem(acc), vmem(spec), *arrays)
    return out.reshape(embed.shape[0], z.emb)


def solution(mesh):
    return jax.shard_map(
        functools.partial(shards, dict(mesh.shape)),
        mesh=mesh,
        in_specs=(
            P(("grp", "hub"), None),
            P(("grp", "hub"), None),
            P(("grp", "hub"), None, None),
            P(("grp", "hub"), None),
            P(("grp", "hub"), None),
            P(("grp", "hub"), None, None),
            P(("grp", "hub")),
        ),
        out_specs=P(("grp", "hub"), None),
        check_vma=False,
    )
```

```python
import functools
import math

import jax
import jax.numpy as jnp
from jax import lax
from jax.experimental import pallas as pl
from jax.experimental.pallas import tpu as pltpu
from jax.sharding import PartitionSpec as P

ORDER = 4
SHIFT = 0.2
THETA = 3.0

UNROLL = 16
BITS = 10
MASK = (1 << BITS) - 1
F32 = jnp.float32
BF16 = jnp.bfloat16


def bessel_scaled(order_index):
    total = 0.0
    for term in range(40):
        total += (THETA / 2.0) ** (2 * term + order_index) / (
            math.factorial(term) * math.factorial(term + order_index)
        )
    return math.exp(-THETA) * total


def coefficients():
    values = [bessel_scaled(0)]
    for order_index in range(1, ORDER + 1):
        values.append(2.0 * (-1.0) ** order_index * bessel_scaled(order_index))
    return values


WEIGHTS = coefficients()


def grp_source(g, e, n):
    return g ^ e if power_of_two(n) else (g - e) % n


def grp_target(g, e, n):
    return g ^ e if power_of_two(n) else (g + e) % n


def power_of_two(n):
    return n & (n - 1) == 0


def vmem(x):
    return pltpu.with_memory_space_constraint(x, pltpu.VMEM)


def hbm(x):
    return pltpu.with_memory_space_constraint(x, pltpu.HBM)


VMEM_SPEC = pl.BlockSpec(memory_space=pltpu.VMEM)
SMEM_SPEC = pl.BlockSpec(memory_space=pltpu.SMEM)
ANY_SPEC = pl.BlockSpec(memory_space=pl.ANY)
PARAMS = pltpu.CompilerParams(vmem_limit_bytes=8 * 1024 * 1024)


class Sizes:
    def __init__(self, mesh_shape, embed, hub_ids, send_ids, tile_val):
        self.n_grp, self.n_hub = mesh_shape["grp"], mesh_shape["hub"]
        self.blk, self.emb = tile_val.shape[1], embed.shape[1]
        self.nb = embed.shape[0] // self.blk
        self.slots = tile_val.shape[0]
        self.hub = hub_ids.shape[1]
        self.tail = send_ids.shape[2]
        self.hub_slots = (self.n_hub - 1) * self.hub
        self.rem = self.hub_slots + (self.n_grp - 1) * self.tail
        self.cap = self.slots + UNROLL
        self.off_local, self.off_first, self.off_rest = 0, self.cap, 2 * self.cap
        self.off_len = 3 * self.cap
        self.off_hub = self.off_len + 3
        self.off_send = self.off_hub + self.hub
        self.list_len = self.off_send + (self.n_grp - 1) * self.tail
        self.tile_flops = 2 * self.blk * self.blk * self.emb
        self.field_bytes = 2 * self.nb * self.blk * self.emb
        assert max(self.slots, self.nb + 1, self.nb + self.rem) <= MASK

    def block(self, n, dtype):
        return jax.ShapeDtypeStruct((n, self.blk, self.emb), dtype)

    def block_vmem(self, n, dtype):
        return pltpu.VMEM((n, self.blk, self.emb), dtype)


def read_scalars(pairs, sems):
    copies = [pltpu.make_async_copy(s, d, sems.at[i]) for i, (s, d) in enumerate(pairs)]
    for c in copies:
        c.start()
    for c in copies:
        c.wait()


def gather_kernel(z, hub_in, send_in, field, hub_out, *rest):
    tails, (hub_ids, send_ids, scalar_sem, sem) = rest[:-4], rest[-4:]
    read_scalars([(hub_in, hub_ids), (send_in, send_ids)], scalar_sem)
    g = lax.axis_index("grp")
    copies = []
    for j in range(z.hub):
        copies.append((field.at[hub_ids[0, j]], hub_out.at[j]))
    for e in range(1, z.n_grp):
        for k in range(z.tail):
            copies.append((field.at[send_ids[0, grp_target(g, e, z.n_grp), k]], tails[e - 1].at[k]))
    copies = [pltpu.make_async_copy(s, d, sem.at[i]) for i, (s, d) in enumerate(copies)]
    for c in copies:
        c.start()
    for c in copies:
        c.wait()


def hub_source(h, d, n):
    return h ^ d if power_of_two(n) else (h - d) % n


def hub_target(h, d, n):
    return h ^ d if power_of_two(n) else (h + d) % n


def bin_kernel(
    z, tile_count, hub_in, send_in, row_in, col_in, vals_in, field_in, lists, vals, field, *scratch
):
    hub_ids, send_ids, tile_row, tile_col, colmap, sent, scalar_sem, sems = scratch
    copies = [
        pltpu.make_async_copy(vals_in, vals, sems.at[0]),
        pltpu.make_async_copy(field_in, field, sems.at[1]),
    ]
    for c in copies:
        c.start()
    read_scalars(
        [(hub_in, hub_ids), (send_in, send_ids), (row_in, tile_row), (col_in, tile_col)],
        scalar_sem,
    )
    g = lax.axis_index("grp")
    mine = lax.axis_index("hub")
    for j in range(z.hub):
        lists[z.off_hub + j] = hub_ids[0, j]
    for e in range(1, z.n_grp):
        for k in range(z.tail):
            lists[z.off_send + (e - 1) * z.tail + k] = send_ids[0, grp_target(g, e, z.n_grp), k]

    def local_cols(i, c):
        sent[i] = 0
        colmap[i] = i
        return c

    lax.fori_loop(0, z.nb, local_cols, 0, unroll=8)
    for j in range(z.hub):
        sent[hub_ids[0, j]] = 1
    for d in range(z.n_hub):
        h = hub_source(mine, d, z.n_hub)
        for j in range(z.hub):
            spot = hub_ids[0, j] if d == 0 else z.nb + (d - 1) * z.hub + j
            colmap[z.nb + h * z.hub + j] = spot
    base = z.nb + z.n_hub * z.hub
    for e in range(z.n_grp):
        src = grp_source(g, e, z.n_grp)
        dst = grp_target(g, e, z.n_grp)
        for k in range(z.tail):
            if e == 0:
                colmap[base + src * z.tail + k] = send_ids[0, g, k]
            else:
                colmap[base + src * z.tail + k] = z.nb + z.hub_slots + (e - 1) * z.tail + k
                sent[send_ids[0, dst, k]] = 1

    total = tile_count[0]
    group = 8 if z.slots % 8 == 0 else 1

    def place(i, counts):
        n0, n1, n2 = counts
        ts = [i * group + u for u in range(group)]
        rows = [tile_row[0, t] for t in ts]
        spots = [colmap[tile_col[0, t]] for t in ts]
        sents = [sent[r] for r in rows]
        entries, places = [], []
        for t, row, spot, out in zip(ts, rows, spots, sents):
            live = (t < total).astype(jnp.int32)
            local = (spot < z.nb).astype(jnp.int32)
            first = (1 - local) * out
            rest = (1 - local) * (1 - out)
            places.append(
                jnp.where(local == 1, z.off_local + n0, jnp.where(first == 1, z.off_first + n1, z.off_rest + n2))
            )
            entries.append(t + (row << BITS) + ((spot - (1 - local) * z.nb) << (2 * BITS)))
            n0, n1, n2 = n0 + local * live, n1 + first * live, n2 + rest * live
        for entry, where in zip(entries, places):
            lists[where] = entry
        return n0, n1, n2

    zero = jnp.int32(0)
    counts = lax.fori_loop(0, (total + group - 1) // group, place, (zero, zero, zero))
    for n, (off, length) in enumerate(zip((z.off_local, z.off_first, z.off_rest), counts)):
        for u in range(UNROLL):
            lists[off + length + u] = z.nb << BITS
        lists[z.off_len + n] = length
    for c in copies:
        c.wait()


def accumulate(z, lists, which, vals, source, acc, scale=None):
    off = (z.off_local, z.off_first, z.off_rest)[which]
    length = lists[z.off_len + which]

    def body(i, c):
        entries = [lists[off + i * UNROLL + u] for u in range(UNROLL)]
        prods = [
            jnp.dot(vals[e & MASK], source[e >> (2 * BITS)], preferred_element_type=F32)
            for e in entries
        ]
        for e, p in zip(entries, prods):
            row = (e >> BITS) & MASK
            acc[row] = acc[row] + (p if scale is None else scale * p)
        return c

    lax.fori_loop(0, (length + UNROLL - 1) // UNROLL, body, 0)


def fetch(parts, refs, rem, sems):
    copies = []
    for i, ((slot, n), ref) in enumerate(zip(parts, refs)):
        copies.append(pltpu.make_async_copy(ref, rem.at[pl.ds(slot, n)], sems.at[i]))
    for c in copies:
        c.start()
    for c in copies:
        c.wait()


def start_kernel(z, lists, vals, field, acc):
    def body(r, c):
        acc[r] = -SHIFT * field[r].astype(F32)
        return c

    lax.fori_loop(0, z.nb, body, 0)
    accumulate(z, lists, 0, vals, field, acc)


def edge_kernel(z, parts, step, lists, vals, prev, acc_in, *rest):
    n = len(parts)
    refs, rest = rest[:n], rest[n:]
    acc, rem, hub_out = rest[:3]
    tails = rest[3:-1]
    fetch(parts, refs, rem, rest[-1])
    accumulate(z, lists, 1, vals, rem, acc)

    def value(row):
        if step == 1:
            return acc[row].astype(BF16)
        return (2.0 * acc[row] - prev[row].astype(F32)).astype(BF16)

    for j in range(z.hub):
        hub_out[j] = value(lists[z.off_hub + j])
    for e in range(1, z.n_grp):
        for k in range(z.tail):
            tails[e - 1][k] = value(lists[z.off_send + (e - 1) * z.tail + k])


def finish_kernel(z, step, lists, vals, rem, *rest):
    fields = rest[:step]
    acc, field = rest[-2:]
    accumulate(z, lists, 2, vals, rem, acc)

    def body(r, c):
        if step == 1:
            t = acc[r].astype(BF16)
        else:
            t = (2.0 * acc[r] - fields[step - 2][r].astype(F32)).astype(BF16)
        field[r] = t
        t = t.astype(F32)
        if step < ORDER - 1:
            acc[r] = -SHIFT * t
        else:
            total = (WEIGHTS[step] - 2.0 * SHIFT * WEIGHTS[ORDER]) * t
            for k in range(step):
                w = WEIGHTS[k] - WEIGHTS[ORDER] * (k == ORDER - 2)
                total = total + w * fields[k][r].astype(F32)
            acc[r] = total
        return c

    lax.fori_loop(0, z.nb, body, 0)


def local_kernel(z, scale, lists, vals, field, acc_in, acc):
    accumulate(z, lists, 0, vals, field, acc, scale)


def last_kernel(z, parts, lists, vals, acc_in, *rest):
    n = len(parts)
    refs, rest = rest[:n], rest[n:]
    acc, out, rem, sems, out_sem = rest
    fetch(parts, refs, rem, sems)
    accumulate(z, lists, 1, vals, rem, acc, 2.0 * WEIGHTS[ORDER])
    accumulate(z, lists, 2, vals, rem, acc, 2.0 * WEIGHTS[ORDER])
    c = pltpu.make_async_copy(acc.at[pl.ds(0, z.nb)], out, out_sem)
    c.start()
    c.wait()


def exchange(z, hub, tails):
    got = {}

    def send(x, d):
        return lax.ppermute(x, "hub", [(i, hub_target(i, d, z.n_hub)) for i in range(z.n_hub)])

    n = z.n_hub
    if power_of_two(n):
        bits = [1 << b for b in range(n.bit_length() - 1)]
        for b in reversed(bits):
            got[b] = send(hub, b)
        others = [d for d in range(1, n) if d not in got]
        for d in sorted(others, key=lambda d: -d):
            held = [b for b in bits if d & b]
            b = held[-1] if len(held) == 2 else held[0]
            got[d] = send(got[b], d ^ b)
    else:
        for d in range(1, n):
            got[d] = send(hub, d)
    arrays = [got[d] for d in range(1, n)]
    parts = [((d - 1) * z.hub, z.hub) for d in range(1, n)]
    for e in range(1, z.n_grp):
        arrays.append(
            lax.ppermute(tails[e - 1], "grp", [(i, grp_target(i, e, z.n_grp)) for i in range(z.n_grp)])
        )
        parts.append((z.hub_slots + (e - 1) * z.tail, z.tail))
    return arrays, tuple(parts)


def cost(z, tiles, nbytes):
    return pl.CostEstimate(
        flops=tiles * z.tile_flops,
        bytes_accessed=nbytes + tiles * 2 * z.blk * (z.blk + 5 * z.emb),
        transcendentals=0,
    )


def shards(mesh_shape, embed, hub_ids, send_ids, tile_row, tile_col, tile_val, tile_count):
    z = Sizes(mesh_shape, embed, hub_ids, send_ids, tile_val)
    ngt = z.n_grp - 1
    field0 = embed.reshape(z.nb, z.blk, z.emb)
    sent_shapes = [z.block(z.hub, BF16)] + [z.block(z.tail, BF16)] * ngt
    hub_ids, send_ids = hbm(hub_ids), hbm(send_ids)

    hub, *tails = pl.pallas_call(
        functools.partial(gather_kernel, z),
        out_shape=sent_shapes,
        in_specs=[ANY_SPEC] * 3,
        out_specs=[ANY_SPEC] * (1 + ngt),
        scratch_shapes=[
            pltpu.SMEM(hub_ids.shape, jnp.int32),
            pltpu.SMEM(send_ids.shape, jnp.int32),
            pltpu.SemaphoreType.DMA((2,)),
            pltpu.SemaphoreType.DMA((z.hub + ngt * z.tail,)),
        ],
        compiler_params=PARAMS,
        name="gather",
    )(hub_ids, send_ids, hbm(field0))
    arrays, parts = exchange(z, hub, tails)

    lists, vals, field = pl.pallas_call(
        functools.partial(bin_kernel, z),
        out_shape=[
            pltpu.SMEM((z.list_len,), jnp.int32),
            pltpu.VMEM(tile_val.shape, BF16),
            z.block_vmem(z.nb, BF16),
        ],
        in_specs=[SMEM_SPEC] + [ANY_SPEC] * 6,
        out_specs=[SMEM_SPEC, VMEM_SPEC, VMEM_SPEC],
        scratch_shapes=[
            pltpu.SMEM(hub_ids.shape, jnp.int32),
            pltpu.SMEM(send_ids.shape, jnp.int32),
            pltpu.SMEM(tile_row.shape, jnp.int32),
            pltpu.SMEM(tile_col.shape, jnp.int32),
            pltpu.SMEM((z.nb + z.n_hub * z.hub + z.n_grp * z.tail,), jnp.int32),
            pltpu.SMEM((z.nb,), jnp.int32),
            pltpu.SemaphoreType.DMA((4,)),
            pltpu.SemaphoreType.DMA((2,)),
        ],
        compiler_params=PARAMS,
        cost_estimate=cost(z, 0, 2 * (2 * z.slots * z.blk * z.blk + z.field_bytes)),
        name="binning",
    )(tile_count, hub_ids, send_ids, hbm(tile_row), hbm(tile_col), hbm(tile_val), hbm(field0))

    acc_shape = z.block_vmem(z.nb + 1, F32)
    vals, field = vmem(vals), vmem(field)
    lists = pltpu.with_memory_space_constraint(lists, pltpu.SMEM)
    acc = pl.pallas_call(
        functools.partial(start_kernel, z),
        out_shape=acc_shape,
        in_specs=[SMEM_SPEC, VMEM_SPEC, VMEM_SPEC],
        out_specs=VMEM_SPEC,
        compiler_params=PARAMS,
        cost_estimate=cost(z, z.slots // 2, 3 * z.field_bytes),
        name="start",
    )(lists, vals, field)

    fields = [field]
    sems = pltpu.SemaphoreType.DMA((len(parts),))
    for step in range(1, ORDER):
        prev = fields[max(step - 2, 0)]
        acc, rem, hub, *tails = pl.pallas_call(
            functools.partial(edge_kernel, z, parts, step),
            out_shape=[acc_shape, z.block_vmem(z.rem, BF16)] + sent_shapes,
            in_specs=[SMEM_SPEC] + [VMEM_SPEC] * 3 + [ANY_SPEC] * len(parts),
            out_specs=[VMEM_SPEC] * (3 + ngt),
            input_output_aliases={3: 0},
            scratch_shapes=[sems],
            compiler_params=PARAMS,
            cost_estimate=cost(z, z.slots // 8, 2 * z.rem * z.blk * z.emb),
            name="edge",
        )(lists, vals, prev, vmem(acc), *arrays)
        arrays, _ = exchange(z, hub, tails)
        acc, new = pl.pallas_call(
            functools.partial(finish_kernel, z, step),
            out_shape=[acc_shape, z.block_vmem(z.nb, BF16)],
            in_specs=[SMEM_SPEC] + [VMEM_SPEC] * (3 + step),
            out_specs=[VMEM_SPEC] * 2,
            input_output_aliases={3 + step: 0},
            compiler_params=PARAMS,
            cost_estimate=cost(z, z.slots // 4, 5 * z.field_bytes),
            name="finish",
        )(lists, vals, vmem(rem), *fields, vmem(acc))
        new = vmem(new)
        fields.append(new)
        acc = pl.pallas_call(
            functools.partial(local_kernel, z, 2.0 * WEIGHTS[ORDER] if step == ORDER - 1 else None),
            out_shape=acc_shape,
            in_specs=[SMEM_SPEC] + [VMEM_SPEC] * 3,
            out_specs=VMEM_SPEC,
            input_output_aliases={3: 0},
            compiler_params=PARAMS,
            cost_estimate=cost(z, z.slots // 2, 0),
            name="local",
        )(lists, vals, new, vmem(acc))

    _, out = pl.pallas_call(
        functools.partial(last_kernel, z, parts),
        out_shape=[acc_shape, z.block(z.nb, F32)],
        in_specs=[SMEM_SPEC] + [VMEM_SPEC] * 2 + [ANY_SPEC] * len(parts),
        out_specs=[VMEM_SPEC, ANY_SPEC],
        input_output_aliases={2: 0},
        scratch_shapes=[pltpu.VMEM((z.rem, z.blk, z.emb), BF16), sems, pltpu.SemaphoreType.DMA(())],
        compiler_params=PARAMS,
        name="last",
    )(lists, vals, vmem(acc), *arrays)
    return out.reshape(embed.shape[0], z.emb)


def solution(mesh):
    return jax.shard_map(
        functools.partial(shards, dict(mesh.shape)),
        mesh=mesh,
        in_specs=(
            P(("grp", "hub"), None),
            P(("grp", "hub"), None),
            P(("grp", "hub"), None, None),
            P(("grp", "hub"), None),
            P(("grp", "hub"), None),
            P(("grp", "hub"), None, None),
            P(("grp", "hub")),
        ),
        out_specs=P(("grp", "hub"), None),
        check_vma=False,
    )
```

```python
import functools
import math

import jax
import jax.numpy as jnp
from jax import lax
from jax.experimental import pallas as pl
from jax.experimental.pallas import tpu as pltpu
from jax.sharding import PartitionSpec as P

ORDER = 4
SHIFT = 0.2
THETA = 3.0

UNROLL = 16
START_SHARE = 0
FINISH_SHARE = 6
BITS = 10
MASK = (1 << BITS) - 1
F32 = jnp.float32
BF16 = jnp.bfloat16


def bessel_scaled(order_index):
    total = 0.0
    for term in range(40):
        total += (THETA / 2.0) ** (2 * term + order_index) / (
            math.factorial(term) * math.factorial(term + order_index)
        )
    return math.exp(-THETA) * total


def coefficients():
    values = [bessel_scaled(0)]
    for order_index in range(1, ORDER + 1):
        values.append(2.0 * (-1.0) ** order_index * bessel_scaled(order_index))
    return values


WEIGHTS = coefficients()


def grp_source(g, e, n):
    return g ^ e if power_of_two(n) else (g - e) % n


def grp_target(g, e, n):
    return g ^ e if power_of_two(n) else (g + e) % n


def power_of_two(n):
    return n & (n - 1) == 0


def vmem(x):
    return pltpu.with_memory_space_constraint(x, pltpu.VMEM)


def hbm(x):
    return pltpu.with_memory_space_constraint(x, pltpu.HBM)


VMEM_SPEC = pl.BlockSpec(memory_space=pltpu.VMEM)
SMEM_SPEC = pl.BlockSpec(memory_space=pltpu.SMEM)
ANY_SPEC = pl.BlockSpec(memory_space=pl.ANY)
PARAMS = pltpu.CompilerParams(vmem_limit_bytes=8 * 1024 * 1024)


def hub_source(h, d, n):
    return h ^ d if power_of_two(n) else (h - d) % n


def hub_target(h, d, n):
    return h ^ d if power_of_two(n) else (h + d) % n


def grp_messages(n):
    if power_of_two(n) and n >= 4:
        return [(1, [1])] + [(e, [e, e + 1]) for e in range(2, n, 2)]
    return [(e, [e]) for e in range(1, n)]


def hub_plan(n, hub):
    if not power_of_two(n):
        return list(range(1, n)), []
    bits = [1 << b for b in range(n.bit_length() - 1)]
    second = {b: [] for b in bits}
    for d in range(n - 1, 0, -1):
        held = [b for b in bits if d & b]
        if len(held) > 2:
            second.setdefault(d ^ held[-1], []).append((d, held[-1], range(hub)))
        elif d == 3:
            second[1].append((3, 2, range(hub // 2)))
            second[2].insert(0, (3, 1, range(hub // 2, hub)))
        elif len(held) == 2:
            second[held[0]].append((d, held[1], range(hub)))
    second = [(via, [p for p in pairs if len(p[2])]) for via, pairs in second.items()]
    return bits[::-1], [(via, pairs) for via, pairs in second if pairs]


class Sizes:
    def __init__(self, mesh_shape, embed, hub_ids, send_ids, tile_val):
        self.n_grp, self.n_hub = mesh_shape["grp"], mesh_shape["hub"]
        self.blk, self.emb = tile_val.shape[1], embed.shape[1]
        self.nb = embed.shape[0] // self.blk
        self.slots = tile_val.shape[0]
        self.hub = hub_ids.shape[1]
        self.tail = send_ids.shape[2]
        self.messages = grp_messages(self.n_grp)
        self.hub_first, self.hub_second = hub_plan(self.n_hub, self.hub)
        self.hub_slot, self.tail_slot = {}, {}
        for d in self.hub_first:
            self.hub_slot[d] = len(self.hub_slot) * self.hub
        used = len(self.hub_slot) * self.hub
        for e in range(1, self.n_grp):
            self.tail_slot[e] = used + (e - 1) * self.tail
        self.rem_first = used + (self.n_grp - 1) * self.tail
        used = self.rem_first
        for d in [d for _, pairs in self.hub_second for d, _, _ in pairs]:
            if d not in self.hub_slot:
                self.hub_slot[d] = used
                used += self.hub
        self.rem = used
        self.cap = self.slots + UNROLL
        self.off = [n * self.cap for n in range(4)]
        self.off_len = 4 * self.cap
        self.off_hub = self.off_len + 4
        self.off_send = self.off_hub + self.hub
        self.list_len = self.off_send + (self.n_grp - 1) * self.tail
        self.tile_flops = 2 * self.blk * self.blk * self.emb
        self.field_bytes = 2 * self.nb * self.blk * self.emb
        assert max(self.slots, self.nb + 1, self.nb + self.rem) <= MASK

    def block(self, n, dtype):
        return jax.ShapeDtypeStruct((n, self.blk, self.emb), dtype)

    def block_vmem(self, n, dtype):
        return pltpu.VMEM((n, self.blk, self.emb), dtype)


def read_scalars(pairs, sems):
    copies = [pltpu.make_async_copy(s, d, sems.at[i]) for i, (s, d) in enumerate(pairs)]
    for c in copies:
        c.start()
    for c in copies:
        c.wait()


def gather_kernel(z, hub_in, send_in, field, hub_out, *rest):
    tails, (hub_ids, send_ids, scalar_sem, sem) = rest[:-4], rest[-4:]
    read_scalars([(hub_in, hub_ids), (send_in, send_ids)], scalar_sem)
    g = lax.axis_index("grp")
    copies = []
    for j in range(z.hub):
        copies.append((field.at[hub_ids[0, j]], hub_out.at[j]))
    for (_, shifts), out in zip(z.messages, tails):
        for i, e in enumerate(shifts):
            for k in range(z.tail):
                copies.append((field.at[send_ids[0, grp_target(g, e, z.n_grp), k]], out.at[i * z.tail + k]))
    copies = [pltpu.make_async_copy(s, d, sem.at[i]) for i, (s, d) in enumerate(copies)]
    for c in copies:
        c.start()
    for c in copies:
        c.wait()


def bin_kernel(
    z, tile_count, hub_in, send_in, row_in, col_in, vals_in, field_in, lists, vals, field, *scratch
):
    hub_ids, send_ids, tile_row, tile_col, colmap, sent, scalar_sem, sems = scratch
    copies = [
        pltpu.make_async_copy(vals_in, vals, sems.at[0]),
        pltpu.make_async_copy(field_in, field, sems.at[1]),
    ]
    for c in copies:
        c.start()
    read_scalars(
        [(hub_in, hub_ids), (send_in, send_ids), (row_in, tile_row), (col_in, tile_col)],
        scalar_sem,
    )
    g = lax.axis_index("grp")
    mine = lax.axis_index("hub")
    for j in range(z.hub):
        lists[z.off_hub + j] = hub_ids[0, j]
    for n, e in enumerate(e for _, shifts in z.messages for e in shifts):
        for k in range(z.tail):
            lists[z.off_send + n * z.tail + k] = send_ids[0, grp_target(g, e, z.n_grp), k]

    def local_cols(i, c):
        sent[i] = 0
        colmap[i] = i
        return c

    lax.fori_loop(0, z.nb, local_cols, 0, unroll=8)
    for j in range(z.hub):
        sent[hub_ids[0, j]] = 1
    for d in range(z.n_hub):
        h = hub_source(mine, d, z.n_hub)
        for j in range(z.hub):
            spot = hub_ids[0, j] if d == 0 else z.nb + z.hub_slot[d] + j
            colmap[z.nb + h * z.hub + j] = spot
    base = z.nb + z.n_hub * z.hub
    for e in range(z.n_grp):
        src = grp_source(g, e, z.n_grp)
        dst = grp_target(g, e, z.n_grp)
        for k in range(z.tail):
            if e == 0:
                colmap[base + src * z.tail + k] = send_ids[0, g, k]
            else:
                colmap[base + src * z.tail + k] = z.nb + z.tail_slot[e] + k
                sent[send_ids[0, dst, k]] = 1

    total = tile_count[0]
    group = 8 if z.slots % 8 == 0 else 1

    def place(i, counts):
        counts = list(counts)
        ts = [i * group + u for u in range(group)]
        rows = [tile_row[0, t] for t in ts]
        spots = [colmap[tile_col[0, t]] for t in ts]
        sents = [sent[r] for r in rows]
        entries, places = [], []
        for t, row, spot, out in zip(ts, rows, spots, sents):
            live = (t < total).astype(jnp.int32)
            second = (spot >= z.nb + z.rem_first).astype(jnp.int32)
            remote = (spot >= z.nb).astype(jnp.int32)
            kinds = [1 - remote, remote - second, second * out, second * (1 - out)]
            where = jnp.int32(0)
            for n, kind in enumerate(kinds):
                where = where + kind * (z.off[n] + counts[n])
                counts[n] = counts[n] + kind * live
            places.append(where)
            spot = spot - remote * z.nb - second * z.rem_first
            entries.append(t + (row << BITS) + (spot << (2 * BITS)))
        for entry, where in zip(entries, places):
            lists[where] = entry
        return tuple(counts)

    zero = jnp.int32(0)
    counts = lax.fori_loop(0, (total + group - 1) // group, place, (zero,) * 4)
    for n, (off, length) in enumerate(zip(z.off, counts)):
        for u in range(UNROLL):
            lists[off + length + u] = z.nb << BITS
        lists[z.off_len + n] = length
    for c in copies:
        c.wait()


def accumulate(z, lists, which, vals, source, acc, scale=None, begin=0, end=16):
    off = z.off[which]
    groups = (lists[z.off_len + which] + UNROLL - 1) // UNROLL

    def body(i, c):
        entries = [lists[off + i * UNROLL + u] for u in range(UNROLL)]
        prods = [
            jnp.dot(vals[e & MASK], source[e >> (2 * BITS)], preferred_element_type=F32)
            for e in entries
        ]
        for e, p in zip(entries, prods):
            row = (e >> BITS) & MASK
            acc[row] = acc[row] + (p if scale is None else scale * p)
        return c

    lax.fori_loop(groups * begin // 16, groups * end // 16, body, 0)


def fetch(parts, refs, rem, sems):
    copies = []
    for i, ((slot, n), ref) in enumerate(zip(parts, refs)):
        copies.append(pltpu.make_async_copy(ref.at[pl.ds(0, n)], rem.at[pl.ds(slot, n)], sems.at[i]))
    for c in copies:
        c.start()
    return copies


def start_kernel(z, lists, vals, field, acc):
    def body(r, c):
        acc[r] = -SHIFT * field[r].astype(F32)
        return c

    lax.fori_loop(0, z.nb, body, 0)
    accumulate(z, lists, 0, vals, field, acc, end=START_SHARE)


def edge_kernel(z, parts, step, lists, vals, prev, acc_in, *rest):
    n = len(parts)
    refs, rest = rest[:n], rest[n:]
    acc, rem, hub_out = rest[:3]
    tails = rest[3:-1]
    for c in fetch(parts, refs, rem, rest[-1]):
        c.wait()
    accumulate(z, lists, 2, vals, rem, acc)

    def value(row):
        if step == 1:
            return acc[row].astype(BF16)
        return (2.0 * acc[row] - prev[row].astype(F32)).astype(BF16)

    for j in range(z.hub):
        hub_out[j] = value(lists[z.off_hub + j])
    n = 0
    for (_, shifts), out in zip(z.messages, tails):
        for k in range(len(shifts) * z.tail):
            out[k] = value(lists[z.off_send + n])
            n += 1


def finish_kernel(z, step, lists, vals, rem, *rest):
    fields = rest[:step]
    acc, field = rest[-2:]
    accumulate(z, lists, 3, vals, rem, acc)

    def body(r, c):
        if step == 1:
            t = acc[r].astype(BF16)
        else:
            t = (2.0 * acc[r] - fields[step - 2][r].astype(F32)).astype(BF16)
        field[r] = t
        t = t.astype(F32)
        if step < ORDER - 1:
            acc[r] = -SHIFT * t
        else:
            total = (WEIGHTS[step] - 2.0 * SHIFT * WEIGHTS[ORDER]) * t
            for k in range(step):
                w = WEIGHTS[k] - WEIGHTS[ORDER] * (k == ORDER - 2)
                total = total + w * fields[k][r].astype(F32)
            acc[r] = total
        return c

    lax.fori_loop(0, z.nb, body, 0)
    accumulate(z, lists, 0, vals, field, acc, step_scale(step), end=FINISH_SHARE)


def step_scale(step):
    return 2.0 * WEIGHTS[ORDER] if step == ORDER - 1 else None


def local_kernel(z, parts, step, lists, vals, field, acc_in, *rest):
    n = len(parts)
    refs, (acc, rem, sems) = rest[:n], rest[n:]
    copies = fetch(parts, refs, rem, sems)
    share = START_SHARE if step == 0 else FINISH_SHARE
    accumulate(z, lists, 0, vals, field, acc, step_scale(step), begin=share)
    for c in copies:
        c.wait()
    accumulate(z, lists, 1, vals, rem, acc, step_scale(step))


def last_kernel(z, parts, lists, vals, acc_in, *rest):
    n = len(parts)
    refs, rest = rest[:n], rest[n:]
    acc, out, rem, sems, out_sem = rest
    for c in fetch(parts, refs, rem, sems):
        c.wait()
    accumulate(z, lists, 2, vals, rem, acc, step_scale(ORDER - 1))
    accumulate(z, lists, 3, vals, rem, acc, step_scale(ORDER - 1))
    c = pltpu.make_async_copy(acc.at[pl.ds(0, z.nb)], out, out_sem)
    c.start()
    c.wait()


def over_hub(z, x, d):
    return lax.ppermute(x, "hub", [(i, hub_target(i, d, z.n_hub)) for i in range(z.n_hub)])


def over_grp(z, x, e):
    return lax.ppermute(x, "grp", [(i, grp_target(i, e, z.n_grp)) for i in range(z.n_grp)])


def first_stage(z, hub, tails):
    got = {d: over_hub(z, hub, d) for d in z.hub_first}
    arrays = [got[d] for d in z.hub_first]
    parts = [(z.hub_slot[d], z.hub) for d in z.hub_first]
    for (e, shifts), tail in zip(z.messages, tails):
        mail = over_grp(z, tail, e)
        arrays.append(mail)
        parts.append((z.tail_slot[shifts[0]], z.tail))
        if len(shifts) == 2:
            arrays.append(over_grp(z, mail[z.tail :], 1))
            parts.append((z.tail_slot[shifts[1]], z.tail))
    return got, arrays, tuple(parts)


def second_stage(z, got):
    arrays, parts = [], []
    for via, pairs in z.hub_second:
        held = [got[b][blocks.start : blocks.stop] for _, b, blocks in pairs]
        held = held[0] if len(held) == 1 else jnp.concatenate(held)
        arrays.append(over_hub(z, held, via))
        d, _, blocks = pairs[0]
        parts.append((z.hub_slot[d] + blocks.start - z.rem_first, held.shape[0]))
    return arrays, tuple(parts)


def cost(z, tiles, nbytes):
    return pl.CostEstimate(
        flops=tiles * z.tile_flops,
        bytes_accessed=nbytes + tiles * 2 * z.blk * (z.blk + 5 * z.emb),
        transcendentals=0,
    )


def shards(mesh_shape, embed, hub_ids, send_ids, tile_row, tile_col, tile_val, tile_count):
    z = Sizes(mesh_shape, embed, hub_ids, send_ids, tile_val)
    field0 = embed.reshape(z.nb, z.blk, z.emb)
    sent_shapes = [z.block(z.hub, BF16)] + [z.block(len(shifts) * z.tail, BF16) for _, shifts in z.messages]
    hub_ids, send_ids = hbm(hub_ids), hbm(send_ids)

    hub, *tails = pl.pallas_call(
        functools.partial(gather_kernel, z),
        out_shape=sent_shapes,
        in_specs=[ANY_SPEC] * 3,
        out_specs=[ANY_SPEC] * len(sent_shapes),
        scratch_shapes=[
            pltpu.SMEM(hub_ids.shape, jnp.int32),
            pltpu.SMEM(send_ids.shape, jnp.int32),
            pltpu.SemaphoreType.DMA((2,)),
            pltpu.SemaphoreType.DMA((z.hub + (z.n_grp - 1) * z.tail,)),
        ],
        compiler_params=PARAMS,
        name="gather",
    )(hub_ids, send_ids, hbm(field0))
    got, arrays, parts = first_stage(z, hub, tails)

    lists, vals, field = pl.pallas_call(
        functools.partial(bin_kernel, z),
        out_shape=[
            pltpu.SMEM((z.list_len,), jnp.int32),
            pltpu.VMEM(tile_val.shape, BF16),
            z.block_vmem(z.nb, BF16),
        ],
        in_specs=[SMEM_SPEC] + [ANY_SPEC] * 6,
        out_specs=[SMEM_SPEC, VMEM_SPEC, VMEM_SPEC],
        scratch_shapes=[
            pltpu.SMEM(hub_ids.shape, jnp.int32),
            pltpu.SMEM(send_ids.shape, jnp.int32),
            pltpu.SMEM(tile_row.shape, jnp.int32),
            pltpu.SMEM(tile_col.shape, jnp.int32),
            pltpu.SMEM((z.nb + z.n_hub * z.hub + z.n_grp * z.tail,), jnp.int32),
            pltpu.SMEM((z.nb,), jnp.int32),
            pltpu.SemaphoreType.DMA((4,)),
            pltpu.SemaphoreType.DMA((2,)),
        ],
        compiler_params=PARAMS,
        cost_estimate=cost(z, 0, 2 * (2 * z.slots * z.blk * z.blk + z.field_bytes)),
        name="binning",
    )(tile_count, hub_ids, send_ids, hbm(tile_row), hbm(tile_col), hbm(tile_val), hbm(field0))

    acc_shape = z.block_vmem(z.nb + 1, F32)
    vals, field = vmem(vals), vmem(field)
    lists = pltpu.with_memory_space_constraint(lists, pltpu.SMEM)
    acc = pl.pallas_call(
        functools.partial(start_kernel, z),
        out_shape=acc_shape,
        in_specs=[SMEM_SPEC, VMEM_SPEC, VMEM_SPEC],
        out_specs=VMEM_SPEC,
        compiler_params=PARAMS,
        cost_estimate=cost(z, z.slots // 2, 3 * z.field_bytes),
        name="start",
    )(lists, vals, field)

    fields = [field]
    for step in range(ORDER):
        if step > 0:
            acc, rem, hub, *tails = pl.pallas_call(
                functools.partial(edge_kernel, z, late_parts, step),
                out_shape=[acc_shape, z.block_vmem(z.rem - z.rem_first, BF16)] + sent_shapes,
                in_specs=[SMEM_SPEC] + [VMEM_SPEC] * 3 + [ANY_SPEC] * len(late_parts),
                out_specs=[VMEM_SPEC] * (2 + len(sent_shapes)),
                input_output_aliases={3: 0},
                scratch_shapes=[pltpu.SemaphoreType.DMA((len(late_parts),))],
                compiler_params=PARAMS,
                cost_estimate=cost(z, z.slots // 16, 2 * z.rem * z.blk * z.emb),
                name="edge",
            )(lists, vals, fields[max(step - 2, 0)], vmem(acc), *late)
            got, arrays, parts = first_stage(z, hub, tails)
            acc, new = pl.pallas_call(
                functools.partial(finish_kernel, z, step),
                out_shape=[acc_shape, z.block_vmem(z.nb, BF16)],
                in_specs=[SMEM_SPEC] + [VMEM_SPEC] * (3 + step),
                out_specs=[VMEM_SPEC] * 2,
                input_output_aliases={3 + step: 0},
                compiler_params=PARAMS,
                cost_estimate=cost(z, z.slots // 4, 5 * z.field_bytes),
                name="finish",
            )(lists, vals, vmem(rem), *fields, vmem(acc))
            fields.append(vmem(new))
        got, acc = lax.optimization_barrier((got, acc))
        late, late_parts = second_stage(z, got)
        acc = pl.pallas_call(
            functools.partial(local_kernel, z, parts, step),
            out_shape=acc_shape,
            in_specs=[SMEM_SPEC] + [VMEM_SPEC] * 3 + [ANY_SPEC] * len(parts),
            out_specs=VMEM_SPEC,
            input_output_aliases={3: 0},
            scratch_shapes=[
                pltpu.VMEM((z.rem_first, z.blk, z.emb), BF16),
                pltpu.SemaphoreType.DMA((len(parts),)),
            ],
            compiler_params=PARAMS,
            cost_estimate=cost(z, z.slots // 2, 0),
            name="local",
        )(lists, vals, fields[-1], vmem(acc), *arrays)

    _, out = pl.pallas_call(
        functools.partial(last_kernel, z, late_parts),
        out_shape=[acc_shape, z.block(z.nb, F32)],
        in_specs=[SMEM_SPEC] + [VMEM_SPEC] * 2 + [ANY_SPEC] * len(late_parts),
        out_specs=[VMEM_SPEC, ANY_SPEC],
        input_output_aliases={2: 0},
        scratch_shapes=[
            pltpu.VMEM((z.rem - z.rem_first, z.blk, z.emb), BF16),
            pltpu.SemaphoreType.DMA((len(late_parts),)),
            pltpu.SemaphoreType.DMA(()),
        ],
        compiler_params=PARAMS,
        name="last",
    )(lists, vals, vmem(acc), *late)
    return out.reshape(embed.shape[0], z.emb)


def solution(mesh):
    return jax.shard_map(
        functools.partial(shards, dict(mesh.shape)),
        mesh=mesh,
        in_specs=(
            P(("grp", "hub"), None),
            P(("grp", "hub"), None),
            P(("grp", "hub"), None, None),
            P(("grp", "hub"), None),
            P(("grp", "hub"), None),
            P(("grp", "hub"), None, None),
            P(("grp", "hub")),
        ),
        out_specs=P(("grp", "hub"), None),
        check_vma=False,
    )
```

```python
import functools
import math

import jax
import jax.numpy as jnp
from jax import lax
from jax.experimental import pallas as pl
from jax.experimental.pallas import tpu as pltpu
from jax.sharding import PartitionSpec as P

ORDER = 4
SHIFT = 0.2
THETA = 3.0

UNROLL = 16
FINISH_SHARE = (0, 6, 6, 0)
BITS = 10
MASK = (1 << BITS) - 1
F32 = jnp.float32
BF16 = jnp.bfloat16


def bessel_scaled(order_index):
    total = 0.0
    for term in range(40):
        total += (THETA / 2.0) ** (2 * term + order_index) / (
            math.factorial(term) * math.factorial(term + order_index)
        )
    return math.exp(-THETA) * total


def coefficients():
    values = [bessel_scaled(0)]
    for order_index in range(1, ORDER + 1):
        values.append(2.0 * (-1.0) ** order_index * bessel_scaled(order_index))
    return values


WEIGHTS = coefficients()


def grp_source(g, e, n):
    return g ^ e if power_of_two(n) else (g - e) % n


def grp_target(g, e, n):
    return g ^ e if power_of_two(n) else (g + e) % n


def power_of_two(n):
    return n & (n - 1) == 0


def vmem(x):
    return pltpu.with_memory_space_constraint(x, pltpu.VMEM)


def hbm(x):
    return pltpu.with_memory_space_constraint(x, pltpu.HBM)


VMEM_SPEC = pl.BlockSpec(memory_space=pltpu.VMEM)
SMEM_SPEC = pl.BlockSpec(memory_space=pltpu.SMEM)
ANY_SPEC = pl.BlockSpec(memory_space=pl.ANY)
PARAMS = pltpu.CompilerParams(vmem_limit_bytes=8 * 1024 * 1024)


def hub_source(h, d, n):
    return h ^ d if power_of_two(n) else (h - d) % n


def hub_target(h, d, n):
    return h ^ d if power_of_two(n) else (h + d) % n


def grp_messages(n):
    if power_of_two(n) and n >= 4:
        return [(1, [1])] + [(e, [e, e + 1]) for e in range(2, n, 2)]
    return [(e, [e]) for e in range(1, n)]


def hub_plan(n, hub):
    if not power_of_two(n):
        return list(range(1, n)), []
    bits = [1 << b for b in range(n.bit_length() - 1)]
    second = {b: [] for b in bits}
    for d in range(n - 1, 0, -1):
        held = [b for b in bits if d & b]
        if len(held) > 2:
            second.setdefault(d ^ held[-1], []).append((d, held[-1], range(hub)))
        elif d == 3:
            second[1].append((3, 2, range(hub // 2)))
            second[2].insert(0, (3, 1, range(hub // 2, hub)))
        elif len(held) == 2:
            second[held[0]].append((d, held[1], range(hub)))
    second = [(via, [p for p in pairs if len(p[2])]) for via, pairs in second.items()]
    return bits[::-1], [(via, pairs) for via, pairs in second if pairs]


class Sizes:
    def __init__(self, mesh_shape, embed, hub_ids, send_ids, tile_val):
        self.n_grp, self.n_hub = mesh_shape["grp"], mesh_shape["hub"]
        self.blk, self.emb = tile_val.shape[1], embed.shape[1]
        self.nb = embed.shape[0] // self.blk
        self.slots = tile_val.shape[0]
        self.hub = hub_ids.shape[1]
        self.tail = send_ids.shape[2]
        self.messages = grp_messages(self.n_grp)
        self.hub_first, self.hub_second = hub_plan(self.n_hub, self.hub)
        self.hub_slot, self.tail_slot = {}, {}
        for d in self.hub_first:
            self.hub_slot[d] = len(self.hub_slot) * self.hub
        used = len(self.hub_slot) * self.hub
        for e in range(1, self.n_grp):
            self.tail_slot[e] = used + (e - 1) * self.tail
        self.rem_first = used + (self.n_grp - 1) * self.tail
        used = self.rem_first
        for d in [d for _, pairs in self.hub_second for d, _, _ in pairs]:
            if d not in self.hub_slot:
                self.hub_slot[d] = used
                used += self.hub
        self.rem = used
        self.cap = self.slots + UNROLL
        self.off_local, self.off_first, self.middle = 0, self.cap, 3 * self.cap
        self.off_len = 4 * self.cap
        self.off_hub = self.off_len + 4
        self.off_send = self.off_hub + self.hub
        self.list_len = self.off_send + (self.n_grp - 1) * self.tail
        self.tile_flops = 2 * self.blk * self.blk * self.emb
        self.field_bytes = 2 * self.nb * self.blk * self.emb
        assert max(self.slots, self.nb + 1, self.nb + self.rem) <= MASK

    def remote_code(self, slot):
        if slot < self.rem_first:
            return (slot << (2 * BITS)) + 1
        return ((slot - self.rem_first) << (2 * BITS)) + 2

    def block(self, n, dtype):
        return jax.ShapeDtypeStruct((n, self.blk, self.emb), dtype)

    def block_vmem(self, n, dtype):
        return pltpu.VMEM((n, self.blk, self.emb), dtype)


def read_scalars(pairs, sems):
    copies = [pltpu.make_async_copy(s, d, sems.at[i]) for i, (s, d) in enumerate(pairs)]
    for c in copies:
        c.start()
    for c in copies:
        c.wait()


def gather_kernel(z, hub_in, send_in, field, field_out, hub_out, *rest):
    tails, (hub_ids, send_ids, scalar_sem, sem, field_sem) = rest[:-5], rest[-5:]
    whole = pltpu.make_async_copy(field, field_out, field_sem)
    whole.start()
    read_scalars([(hub_in, hub_ids), (send_in, send_ids)], scalar_sem)
    g = lax.axis_index("grp")
    copies = []
    for j in range(z.hub):
        copies.append((field.at[hub_ids[0, j]], hub_out.at[j]))
    for (_, shifts), out in zip(z.messages, tails):
        for i, e in enumerate(shifts):
            for k in range(z.tail):
                copies.append((field.at[send_ids[0, grp_target(g, e, z.n_grp), k]], out.at[i * z.tail + k]))
    copies = [pltpu.make_async_copy(s, d, sem.at[i]) for i, (s, d) in enumerate(copies)]
    for c in copies:
        c.start()
    for c in copies:
        c.wait()
    whole.wait()


def bin_kernel(
    z, tile_count, hub_in, send_in, row_in, col_in, vals_in, lists, vals, *scratch
):
    hub_ids, send_ids, tile_row, tile_col, colmap, unsent, ends, scalar_sem, load_sem = scratch
    load = pltpu.make_async_copy(vals_in, vals, load_sem)
    load.start()
    read_scalars(
        [(hub_in, hub_ids), (send_in, send_ids), (row_in, tile_row), (col_in, tile_col)],
        scalar_sem,
    )
    g = lax.axis_index("grp")
    mine = lax.axis_index("hub")
    for j in range(z.hub):
        lists[z.off_hub + j] = hub_ids[0, j]
    for n, e in enumerate(e for _, shifts in z.messages for e in shifts):
        for k in range(z.tail):
            lists[z.off_send + n * z.tail + k] = send_ids[0, grp_target(g, e, z.n_grp), k]

    def local_cols(i, c):
        unsent[i] = 1
        colmap[i] = i << (2 * BITS)
        return c

    lax.fori_loop(0, z.nb, local_cols, 0, unroll=8)
    for j in range(z.hub):
        unsent[hub_ids[0, j]] = 0
    for d in range(z.n_hub):
        h = hub_source(mine, d, z.n_hub)
        for j in range(z.hub):
            code = hub_ids[0, j] << (2 * BITS) if d == 0 else z.remote_code(z.hub_slot[d] + j)
            colmap[z.nb + h * z.hub + j] = code
    base = z.nb + z.n_hub * z.hub
    for e in range(z.n_grp):
        src = grp_source(g, e, z.n_grp)
        dst = grp_target(g, e, z.n_grp)
        for k in range(z.tail):
            if e == 0:
                colmap[base + src * z.tail + k] = send_ids[0, g, k] << (2 * BITS)
            else:
                colmap[base + src * z.tail + k] = z.remote_code(z.tail_slot[e] + k)
                unsent[send_ids[0, dst, k]] = 0

    total = tile_count[0]
    group = 8 if z.slots % 8 == 0 else 1

    starts = (z.off_local, z.off_first, z.middle, z.middle - 1)
    for n, start in enumerate(starts):
        ends[n] = start

    def place(i, c):
        ts = [i * group + u for u in range(group)]
        rows = [tile_row[0, t] for t in ts]
        codes = [colmap[tile_col[0, t]] for t in ts]
        others = [unsent[r] for r in rows]
        for t, row, code, other in zip(ts, rows, codes, others):
            stage = code & 3
            kind = stage + ((stage >> 1) & other)
            step = (t < total).astype(jnp.int32)
            end = ends[kind]
            lists[end] = (code - stage) + (row << BITS) + t
            ends[kind] = end + jnp.where(kind == 3, -step, step)
        return c

    lax.fori_loop(0, (total + group - 1) // group, place, 0)
    for n, start in enumerate(starts):
        end = ends[n]
        for u in range(UNROLL):
            lists[end + u if n < 3 else end - u] = z.nb << BITS
        lists[z.off_len + n] = end - start if n < 3 else start - end
    load.wait()


def accumulate(z, lists, which, vals, source, acc, scale=None, begin=0, end=16):
    if which == 4:
        length = lists[z.off_len + 2] + lists[z.off_len + 3]
    else:
        length = lists[z.off_len + which]
    groups = (length + UNROLL - 1) // UNROLL
    if which < 3:
        off = (z.off_local, z.off_first, z.middle)[which]
    else:
        off = z.middle - (groups * UNROLL if which == 3 else lists[z.off_len + 3])

    def body(i, c):
        entries = [lists[off + i * UNROLL + u] for u in range(UNROLL)]
        prods = [
            jnp.dot(vals[e & MASK], source[e >> (2 * BITS)], preferred_element_type=F32)
            for e in entries
        ]
        for e, p in zip(entries, prods):
            row = (e >> BITS) & MASK
            acc[row] = acc[row] + (p if scale is None else scale * p)
        return c

    lax.fori_loop(groups * begin // 16, groups * end // 16, body, 0)


def fetch(parts, refs, rem):
    for (slot, n), ref in zip(parts, refs):
        for i in range(n):
            rem[slot + i] = ref[i]


def start_kernel(z, lists, vals, field, acc):
    def body(r, c):
        acc[r] = -SHIFT * field[r].astype(F32)
        return c

    lax.fori_loop(0, z.nb, body, 0)


def edge_kernel(z, parts, step, lists, vals, prev, acc_in, *rest):
    n = len(parts)
    refs, rest = rest[:n], rest[n:]
    acc, rem, hub_out = rest[:3]
    tails = rest[3:]
    fetch(parts, refs, rem)
    accumulate(z, lists, 2, vals, rem, acc)

    def value(row):
        if step == 1:
            return acc[row].astype(BF16)
        return (2.0 * acc[row] - prev[row].astype(F32)).astype(BF16)

    for j in range(z.hub):
        hub_out[j] = value(lists[z.off_hub + j])
    n = 0
    for (_, shifts), out in zip(z.messages, tails):
        for k in range(len(shifts) * z.tail):
            out[k] = value(lists[z.off_send + n])
            n += 1


def finish_kernel(z, step, lists, vals, rem, *rest):
    fields = rest[:step]
    acc, field = rest[-2:]
    accumulate(z, lists, 3, vals, rem, acc)

    def body(r, c):
        if step == 1:
            t = acc[r].astype(BF16)
        else:
            t = (2.0 * acc[r] - fields[step - 2][r].astype(F32)).astype(BF16)
        field[r] = t
        t = t.astype(F32)
        if step < ORDER - 1:
            acc[r] = -SHIFT * t
        else:
            total = (WEIGHTS[step] - 2.0 * SHIFT * WEIGHTS[ORDER]) * t
            for k in range(step):
                w = WEIGHTS[k] - WEIGHTS[ORDER] * (k == ORDER - 2)
                total = total + w * fields[k][r].astype(F32)
            acc[r] = total
        return c

    lax.fori_loop(0, z.nb, body, 0)
    accumulate(z, lists, 0, vals, field, acc, step_scale(step), end=FINISH_SHARE[step])


def step_scale(step):
    return 2.0 * WEIGHTS[ORDER] if step == ORDER - 1 else None


def local_kernel(z, parts, step, lists, vals, field, acc_in, *rest):
    n = len(parts)
    refs, (acc, rem) = rest[:n], rest[n:]
    share = FINISH_SHARE[step]
    accumulate(z, lists, 0, vals, field, acc, step_scale(step), begin=share)
    fetch(parts, refs, rem)
    accumulate(z, lists, 1, vals, rem, acc, step_scale(step))


def last_kernel(z, parts, lists, vals, acc_in, *rest):
    n = len(parts)
    refs, rest = rest[:n], rest[n:]
    acc, out, rem, out_sem = rest
    fetch(parts, refs, rem)
    accumulate(z, lists, 4, vals, rem, acc, step_scale(ORDER - 1))
    c = pltpu.make_async_copy(acc.at[pl.ds(0, z.nb)], out, out_sem)
    c.start()
    c.wait()


def over_hub(z, x, d):
    return lax.ppermute(x, "hub", [(i, hub_target(i, d, z.n_hub)) for i in range(z.n_hub)])


def over_grp(z, x, e):
    return lax.ppermute(x, "grp", [(i, grp_target(i, e, z.n_grp)) for i in range(z.n_grp)])


def first_stage(z, hub, tails):
    got = {d: over_hub(z, hub, d) for d in z.hub_first}
    arrays = [got[d] for d in z.hub_first]
    parts = [(z.hub_slot[d], z.hub) for d in z.hub_first]
    for (e, shifts), tail in zip(z.messages, tails):
        mail = over_grp(z, tail, e)
        arrays.append(mail)
        parts.append((z.tail_slot[shifts[0]], z.tail))
        if len(shifts) == 2:
            arrays.append(over_grp(z, mail[z.tail :], 1))
            parts.append((z.tail_slot[shifts[1]], z.tail))
    return got, arrays, tuple(parts)


def second_stage(z, got):
    arrays, parts = [], []
    for via, pairs in z.hub_second:
        held = [got[b][blocks.start : blocks.stop] for _, b, blocks in pairs]
        held = held[0] if len(held) == 1 else jnp.concatenate(held)
        arrays.append(over_hub(z, held, via))
        d, _, blocks = pairs[0]
        parts.append((z.hub_slot[d] + blocks.start - z.rem_first, held.shape[0]))
    return arrays, tuple(parts)


def cost(z, tiles, nbytes):
    return pl.CostEstimate(
        flops=tiles * z.tile_flops,
        bytes_accessed=nbytes + tiles * 2 * z.blk * (z.blk + 5 * z.emb),
        transcendentals=0,
    )


def shards(mesh_shape, embed, hub_ids, send_ids, tile_row, tile_col, tile_val, tile_count):
    z = Sizes(mesh_shape, embed, hub_ids, send_ids, tile_val)
    field0 = embed.reshape(z.nb, z.blk, z.emb)
    sent_shapes = [z.block(z.hub, BF16)] + [z.block(len(shifts) * z.tail, BF16) for _, shifts in z.messages]
    hub_ids, send_ids = hbm(hub_ids), hbm(send_ids)

    field, hub, *tails = pl.pallas_call(
        functools.partial(gather_kernel, z),
        out_shape=[z.block_vmem(z.nb, BF16)] + sent_shapes,
        in_specs=[ANY_SPEC] * 3,
        out_specs=[VMEM_SPEC] + [ANY_SPEC] * len(sent_shapes),
        scratch_shapes=[
            pltpu.SMEM(hub_ids.shape, jnp.int32),
            pltpu.SMEM(send_ids.shape, jnp.int32),
            pltpu.SemaphoreType.DMA((2,)),
            pltpu.SemaphoreType.DMA((z.hub + (z.n_grp - 1) * z.tail,)),
            pltpu.SemaphoreType.DMA(()),
        ],
        compiler_params=PARAMS,
        name="gather",
    )(hub_ids, send_ids, hbm(field0))
    got, arrays, parts = first_stage(z, hub, tails)

    lists, vals = pl.pallas_call(
        functools.partial(bin_kernel, z),
        out_shape=[
            pltpu.SMEM((z.list_len,), jnp.int32),
            pltpu.VMEM(tile_val.shape, BF16),
        ],
        in_specs=[SMEM_SPEC] + [ANY_SPEC] * 5,
        out_specs=[SMEM_SPEC, VMEM_SPEC],
        scratch_shapes=[
            pltpu.SMEM(hub_ids.shape, jnp.int32),
            pltpu.SMEM(send_ids.shape, jnp.int32),
            pltpu.SMEM(tile_row.shape, jnp.int32),
            pltpu.SMEM(tile_col.shape, jnp.int32),
            pltpu.SMEM((z.nb + z.n_hub * z.hub + z.n_grp * z.tail,), jnp.int32),
            pltpu.SMEM((z.nb,), jnp.int32),
            pltpu.SMEM((4,), jnp.int32),
            pltpu.SemaphoreType.DMA((4,)),
            pltpu.SemaphoreType.DMA(()),
        ],
        compiler_params=PARAMS,
        cost_estimate=cost(z, 0, 2 * (2 * z.slots * z.blk * z.blk + z.field_bytes)),
        name="binning",
    )(tile_count, hub_ids, send_ids, hbm(tile_row), hbm(tile_col), hbm(tile_val))

    acc_shape = z.block_vmem(z.nb + 1, F32)
    vals, field = vmem(vals), vmem(field)
    lists = pltpu.with_memory_space_constraint(lists, pltpu.SMEM)
    acc = pl.pallas_call(
        functools.partial(start_kernel, z),
        out_shape=acc_shape,
        in_specs=[SMEM_SPEC, VMEM_SPEC, VMEM_SPEC],
        out_specs=VMEM_SPEC,
        compiler_params=PARAMS,
        cost_estimate=cost(z, z.slots // 2, 3 * z.field_bytes),
        name="start",
    )(lists, vals, field)

    fields = [field]
    for step in range(ORDER):
        if step > 0:
            acc, rem, hub, *tails = pl.pallas_call(
                functools.partial(edge_kernel, z, late_parts, step),
                out_shape=[acc_shape, z.block_vmem(z.rem - z.rem_first, BF16)] + sent_shapes,
                in_specs=[SMEM_SPEC] + [VMEM_SPEC] * (3 + len(late_parts)),
                out_specs=[VMEM_SPEC] * (2 + len(sent_shapes)),
                input_output_aliases={3: 0},
                compiler_params=PARAMS,
                cost_estimate=cost(z, z.slots // 16, 2 * z.rem * z.blk * z.emb),
                name="edge",
            )(lists, vals, fields[max(step - 2, 0)], vmem(acc), *map(vmem, late))
            got, arrays, parts = first_stage(z, hub, tails)
            acc, new = pl.pallas_call(
                functools.partial(finish_kernel, z, step),
                out_shape=[acc_shape, z.block_vmem(z.nb, BF16)],
                in_specs=[SMEM_SPEC] + [VMEM_SPEC] * (3 + step),
                out_specs=[VMEM_SPEC] * 2,
                input_output_aliases={3 + step: 0},
                compiler_params=PARAMS,
                cost_estimate=cost(z, z.slots // 4, 5 * z.field_bytes),
                name="finish",
            )(lists, vals, vmem(rem), *fields, vmem(acc))
            fields.append(vmem(new))
        if step == 0:
            got, vals = lax.optimization_barrier((got, vals))
            vals = vmem(vals)
        else:
            got, acc = lax.optimization_barrier((got, acc))
        late, late_parts = second_stage(z, got)
        acc = pl.pallas_call(
            functools.partial(local_kernel, z, parts, step),
            out_shape=acc_shape,
            in_specs=[SMEM_SPEC] + [VMEM_SPEC] * (3 + len(parts)),
            out_specs=VMEM_SPEC,
            input_output_aliases={3: 0},
            scratch_shapes=[pltpu.VMEM((z.rem_first, z.blk, z.emb), BF16)],
            compiler_params=PARAMS,
            cost_estimate=cost(z, z.slots // 2, 0),
            name="local",
        )(lists, vals, fields[-1], vmem(acc), *map(vmem, arrays))

    _, out = pl.pallas_call(
        functools.partial(last_kernel, z, late_parts),
        out_shape=[acc_shape, z.block(z.nb, F32)],
        in_specs=[SMEM_SPEC] + [VMEM_SPEC] * (2 + len(late_parts)),
        out_specs=[VMEM_SPEC, ANY_SPEC],
        input_output_aliases={2: 0},
        scratch_shapes=[
            pltpu.VMEM((z.rem - z.rem_first, z.blk, z.emb), BF16),
            pltpu.SemaphoreType.DMA(()),
        ],
        compiler_params=PARAMS,
        name="last",
    )(lists, vals, vmem(acc), *map(vmem, late))
    return out.reshape(embed.shape[0], z.emb)


def solution(mesh):
    return jax.shard_map(
        functools.partial(shards, dict(mesh.shape)),
        mesh=mesh,
        in_specs=(
            P(("grp", "hub"), None),
            P(("grp", "hub"), None),
            P(("grp", "hub"), None, None),
            P(("grp", "hub"), None),
            P(("grp", "hub"), None),
            P(("grp", "hub"), None, None),
            P(("grp", "hub")),
        ),
        out_specs=P(("grp", "hub"), None),
        check_vma=False,
    )
```

```python
import functools
import math

import jax
import jax.numpy as jnp
from jax import lax
from jax.experimental import pallas as pl
from jax.experimental.pallas import tpu as pltpu
from jax.sharding import PartitionSpec as P

ORDER = 4
SHIFT = 0.2
THETA = 3.0

UNROLL = 16
FINISH_SHARE = (0, 6, 6, 0)
BITS = 10
MASK = (1 << BITS) - 1
F32 = jnp.float32
BF16 = jnp.bfloat16


def bessel_scaled(order_index):
    total = 0.0
    for term in range(40):
        total += (THETA / 2.0) ** (2 * term + order_index) / (
            math.factorial(term) * math.factorial(term + order_index)
        )
    return math.exp(-THETA) * total


def coefficients():
    values = [bessel_scaled(0)]
    for order_index in range(1, ORDER + 1):
        values.append(2.0 * (-1.0) ** order_index * bessel_scaled(order_index))
    return values


WEIGHTS = coefficients()


def grp_source(g, e, n):
    return g ^ e if power_of_two(n) else (g - e) % n


def grp_target(g, e, n):
    return g ^ e if power_of_two(n) else (g + e) % n


def power_of_two(n):
    return n & (n - 1) == 0


def vmem(x):
    return pltpu.with_memory_space_constraint(x, pltpu.VMEM)


def hbm(x):
    return pltpu.with_memory_space_constraint(x, pltpu.HBM)


VMEM_SPEC = pl.BlockSpec(memory_space=pltpu.VMEM)
SMEM_SPEC = pl.BlockSpec(memory_space=pltpu.SMEM)
ANY_SPEC = pl.BlockSpec(memory_space=pl.ANY)
PARAMS = pltpu.CompilerParams(vmem_limit_bytes=8 * 1024 * 1024)


def hub_source(h, d, n):
    return h ^ d if power_of_two(n) else (h - d) % n


def hub_target(h, d, n):
    return h ^ d if power_of_two(n) else (h + d) % n


def grp_messages(n):
    if power_of_two(n) and n >= 4:
        return [(1, [1])] + [(e, [e, e + 1]) for e in range(2, n, 2)]
    return [(e, [e]) for e in range(1, n)]


def hub_plan(n, hub):
    if not power_of_two(n):
        return list(range(1, n)), []
    bits = [1 << b for b in range(n.bit_length() - 1)]
    second = {b: [] for b in bits}
    for d in range(n - 1, 0, -1):
        held = [b for b in bits if d & b]
        if len(held) > 2:
            second.setdefault(d ^ held[-1], []).append((d, held[-1], range(hub)))
        elif d == 3:
            second[1].append((3, 2, range(hub // 2)))
            second[2].insert(0, (3, 1, range(hub // 2, hub)))
        elif len(held) == 2:
            second[held[0]].append((d, held[1], range(hub)))
    second = [(via, [p for p in pairs if len(p[2])]) for via, pairs in second.items()]
    return bits[::-1], [(via, pairs) for via, pairs in second if pairs]


class Sizes:
    def __init__(self, mesh_shape, embed, hub_ids, send_ids, tile_val):
        self.n_grp, self.n_hub = mesh_shape["grp"], mesh_shape["hub"]
        self.blk, self.emb = tile_val.shape[1], embed.shape[1]
        self.nb = embed.shape[0] // self.blk
        self.slots = tile_val.shape[0]
        self.hub = hub_ids.shape[1]
        self.tail = send_ids.shape[2]
        self.messages = grp_messages(self.n_grp)
        self.hub_first, self.hub_second = hub_plan(self.n_hub, self.hub)
        self.hub_slot, self.tail_slot = {}, {}
        for d in self.hub_first:
            self.hub_slot[d] = len(self.hub_slot) * self.hub
        used = len(self.hub_slot) * self.hub
        for e in range(1, self.n_grp):
            self.tail_slot[e] = used + (e - 1) * self.tail
        self.rem_first = used + (self.n_grp - 1) * self.tail
        used = self.rem_first
        for d in [d for _, pairs in self.hub_second for d, _, _ in pairs]:
            if d not in self.hub_slot:
                self.hub_slot[d] = used
                used += self.hub
        self.rem = used
        self.cap = self.slots + UNROLL
        self.off_local, self.off_first, self.middle = 0, self.cap, 3 * self.cap
        self.off_len = 4 * self.cap
        self.off_hub = self.off_len + 4
        self.off_send = self.off_hub + self.hub
        self.list_len = self.off_send + (self.n_grp - 1) * self.tail
        self.tile_flops = 2 * self.blk * self.blk * self.emb
        self.field_bytes = 2 * self.nb * self.blk * self.emb
        assert max(self.slots, self.nb + 1, self.nb + self.rem) <= MASK

    def remote_code(self, slot):
        if slot < self.rem_first:
            return (slot << (2 * BITS)) + 1
        return ((slot - self.rem_first) << (2 * BITS)) + 2

    def block(self, n, dtype):
        return jax.ShapeDtypeStruct((n, self.blk, self.emb), dtype)

    def block_vmem(self, n, dtype):
        return pltpu.VMEM((n, self.blk, self.emb), dtype)


def read_scalars(pairs, sems):
    copies = [pltpu.make_async_copy(s, d, sems.at[i]) for i, (s, d) in enumerate(pairs)]
    for c in copies:
        c.start()
    for c in copies:
        c.wait()


def gather_kernel(z, hub_in, send_in, field, hub_out, *rest):
    tails, (hub_ids, send_ids, scalar_sem, sem) = rest[:-4], rest[-4:]
    read_scalars([(hub_in, hub_ids), (send_in, send_ids)], scalar_sem)
    g = lax.axis_index("grp")
    copies = []
    for j in range(z.hub):
        copies.append((field.at[hub_ids[0, j]], hub_out.at[j]))
    for (_, shifts), out in zip(z.messages, tails):
        for i, e in enumerate(shifts):
            for k in range(z.tail):
                copies.append((field.at[send_ids[0, grp_target(g, e, z.n_grp), k]], out.at[i * z.tail + k]))
    copies = [pltpu.make_async_copy(s, d, sem.at[i]) for i, (s, d) in enumerate(copies)]
    for c in copies:
        c.start()
    for c in copies:
        c.wait()


def bin_kernel(
    z, tile_count, hub_in, send_in, row_in, col_in, vals_in, field_in, lists, vals, field, *scratch
):
    hub_ids, send_ids, tile_row, tile_col, colmap, unsent, ends, scalar_sem, load_sem = scratch
    loads = [
        pltpu.make_async_copy(vals_in, vals, load_sem.at[0]),
        pltpu.make_async_copy(field_in, field, load_sem.at[1]),
    ]
    for c in loads:
        c.start()
    read_scalars(
        [(hub_in, hub_ids), (send_in, send_ids), (row_in, tile_row), (col_in, tile_col)],
        scalar_sem,
    )
    g = lax.axis_index("grp")
    mine = lax.axis_index("hub")
    for j in range(z.hub):
        lists[z.off_hub + j] = hub_ids[0, j]
    for n, e in enumerate(e for _, shifts in z.messages for e in shifts):
        for k in range(z.tail):
            lists[z.off_send + n * z.tail + k] = send_ids[0, grp_target(g, e, z.n_grp), k]

    def local_cols(i, c):
        unsent[i] = 1
        colmap[i] = i << (2 * BITS)
        return c

    lax.fori_loop(0, z.nb, local_cols, 0, unroll=8)
    for j in range(z.hub):
        unsent[hub_ids[0, j]] = 0
    for d in range(z.n_hub):
        h = hub_source(mine, d, z.n_hub)
        for j in range(z.hub):
            code = hub_ids[0, j] << (2 * BITS) if d == 0 else z.remote_code(z.hub_slot[d] + j)
            colmap[z.nb + h * z.hub + j] = code
    base = z.nb + z.n_hub * z.hub
    for e in range(z.n_grp):
        src = grp_source(g, e, z.n_grp)
        dst = grp_target(g, e, z.n_grp)
        for k in range(z.tail):
            if e == 0:
                colmap[base + src * z.tail + k] = send_ids[0, g, k] << (2 * BITS)
            else:
                colmap[base + src * z.tail + k] = z.remote_code(z.tail_slot[e] + k)
                unsent[send_ids[0, dst, k]] = 0

    total = tile_count[0]
    group = 8 if z.slots % 8 == 0 else 1

    starts = (z.off_local, z.off_first, z.middle, z.middle - 1)
    for n, start in enumerate(starts):
        ends[n] = start

    def place(i, c):
        ts = [i * group + u for u in range(group)]
        rows = [tile_row[0, t] for t in ts]
        codes = [colmap[tile_col[0, t]] for t in ts]
        others = [unsent[r] for r in rows]
        for t, row, code, other in zip(ts, rows, codes, others):
            stage = code & 3
            kind = stage + ((stage >> 1) & other)
            step = (t < total).astype(jnp.int32)
            end = ends[kind]
            lists[end] = (code - stage) + (row << BITS) + t
            ends[kind] = end + jnp.where(kind == 3, -step, step)
        return c

    lax.fori_loop(0, (total + group - 1) // group, place, 0)
    for n, start in enumerate(starts):
        end = ends[n]
        for u in range(UNROLL):
            lists[end + u if n < 3 else end - u] = z.nb << BITS
        lists[z.off_len + n] = end - start if n < 3 else start - end
    for c in loads:
        c.wait()


def accumulate(z, lists, which, vals, source, acc, scale=None, begin=0, end=16):
    if which == 4:
        length = lists[z.off_len + 2] + lists[z.off_len + 3]
    else:
        length = lists[z.off_len + which]
    groups = (length + UNROLL - 1) // UNROLL
    if which < 3:
        off = (z.off_local, z.off_first, z.middle)[which]
    else:
        off = z.middle - (groups * UNROLL if which == 3 else lists[z.off_len + 3])

    def body(i, c):
        entries = [lists[off + i * UNROLL + u] for u in range(UNROLL)]
        prods = [
            jnp.dot(vals[e & MASK], source[e >> (2 * BITS)], preferred_element_type=F32)
            for e in entries
        ]
        for e, p in zip(entries, prods):
            row = (e >> BITS) & MASK
            acc[row] = acc[row] + (p if scale is None else scale * p)
        return c

    lax.fori_loop(groups * begin // 16, groups * end // 16, body, 0)


def fetch(parts, refs, rem):
    for (slot, n), ref in zip(parts, refs):
        for i in range(n):
            rem[slot + i] = ref[i]


def start_kernel(z, lists, vals, field, acc):
    def body(r, c):
        acc[r] = -SHIFT * field[r].astype(F32)
        return c

    lax.fori_loop(0, z.nb, body, 0)


def edge_kernel(z, parts, step, lists, vals, prev, acc_in, *rest):
    n = len(parts)
    refs, rest = rest[:n], rest[n:]
    acc, rem, hub_out = rest[:3]
    tails = rest[3:]
    fetch(parts, refs, rem)
    accumulate(z, lists, 2, vals, rem, acc)

    def value(row):
        if step == 1:
            return acc[row].astype(BF16)
        return (2.0 * acc[row] - prev[row].astype(F32)).astype(BF16)

    for j in range(z.hub):
        hub_out[j] = value(lists[z.off_hub + j])
    n = 0
    for (_, shifts), out in zip(z.messages, tails):
        for k in range(len(shifts) * z.tail):
            out[k] = value(lists[z.off_send + n])
            n += 1


def finish_kernel(z, step, lists, vals, rem, *rest):
    fields = rest[:step]
    acc, field = rest[-2:]
    accumulate(z, lists, 3, vals, rem, acc)

    def body(r, c):
        if step == 1:
            t = acc[r].astype(BF16)
        else:
            t = (2.0 * acc[r] - fields[step - 2][r].astype(F32)).astype(BF16)
        field[r] = t
        t = t.astype(F32)
        if step < ORDER - 1:
            acc[r] = -SHIFT * t
        else:
            total = (WEIGHTS[step] - 2.0 * SHIFT * WEIGHTS[ORDER]) * t
            for k in range(step):
                w = WEIGHTS[k] - WEIGHTS[ORDER] * (k == ORDER - 2)
                total = total + w * fields[k][r].astype(F32)
            acc[r] = total
        return c

    lax.fori_loop(0, z.nb, body, 0)
    accumulate(z, lists, 0, vals, field, acc, step_scale(step), end=FINISH_SHARE[step])


def step_scale(step):
    return 2.0 * WEIGHTS[ORDER] if step == ORDER - 1 else None


def local_kernel(z, parts, step, lists, vals, field, acc_in, *rest):
    n = len(parts)
    refs, (acc, rem) = rest[:n], rest[n:]
    share = FINISH_SHARE[step]
    accumulate(z, lists, 0, vals, field, acc, step_scale(step), begin=share)
    fetch(parts, refs, rem)
    accumulate(z, lists, 1, vals, rem, acc, step_scale(step))


def last_kernel(z, parts, lists, vals, acc_in, *rest):
    n = len(parts)
    refs, rest = rest[:n], rest[n:]
    acc, out, rem, out_sem = rest
    fetch(parts, refs, rem)
    accumulate(z, lists, 4, vals, rem, acc, step_scale(ORDER - 1))
    c = pltpu.make_async_copy(acc.at[pl.ds(0, z.nb)], out, out_sem)
    c.start()
    c.wait()


def over_hub(z, x, d):
    return lax.ppermute(x, "hub", [(i, hub_target(i, d, z.n_hub)) for i in range(z.n_hub)])


def over_grp(z, x, e):
    return lax.ppermute(x, "grp", [(i, grp_target(i, e, z.n_grp)) for i in range(z.n_grp)])


def first_stage(z, hub, tails):
    got = {d: over_hub(z, hub, d) for d in z.hub_first}
    arrays = [got[d] for d in z.hub_first]
    parts = [(z.hub_slot[d], z.hub) for d in z.hub_first]
    for (e, shifts), tail in zip(z.messages, tails):
        mail = over_grp(z, tail, e)
        arrays.append(mail)
        parts.append((z.tail_slot[shifts[0]], z.tail))
        if len(shifts) == 2:
            arrays.append(over_grp(z, mail[z.tail :], 1))
            parts.append((z.tail_slot[shifts[1]], z.tail))
    return got, arrays, tuple(parts)


def second_stage(z, got):
    arrays, parts = [], []
    for via, pairs in z.hub_second:
        held = [got[b][blocks.start : blocks.stop] for _, b, blocks in pairs]
        held = held[0] if len(held) == 1 else jnp.concatenate(held)
        arrays.append(over_hub(z, held, via))
        d, _, blocks = pairs[0]
        parts.append((z.hub_slot[d] + blocks.start - z.rem_first, held.shape[0]))
    return arrays, tuple(parts)


def cost(z, tiles, nbytes):
    return pl.CostEstimate(
        flops=tiles * z.tile_flops,
        bytes_accessed=nbytes + tiles * 2 * z.blk * (z.blk + 5 * z.emb),
        transcendentals=0,
    )


def shards(mesh_shape, embed, hub_ids, send_ids, tile_row, tile_col, tile_val, tile_count):
    z = Sizes(mesh_shape, embed, hub_ids, send_ids, tile_val)
    field0 = embed.reshape(z.nb, z.blk, z.emb)
    sent_shapes = [z.block(z.hub, BF16)] + [z.block(len(shifts) * z.tail, BF16) for _, shifts in z.messages]
    hub_ids, send_ids = hbm(hub_ids), hbm(send_ids)

    hub, *tails = pl.pallas_call(
        functools.partial(gather_kernel, z),
        out_shape=sent_shapes,
        in_specs=[ANY_SPEC] * 3,
        out_specs=[ANY_SPEC] * len(sent_shapes),
        scratch_shapes=[
            pltpu.SMEM(hub_ids.shape, jnp.int32),
            pltpu.SMEM(send_ids.shape, jnp.int32),
            pltpu.SemaphoreType.DMA((2,)),
            pltpu.SemaphoreType.DMA((z.hub + (z.n_grp - 1) * z.tail,)),
        ],
        compiler_params=PARAMS,
        name="gather",
    )(hub_ids, send_ids, hbm(field0))
    got, arrays, parts = first_stage(z, hub, tails)

    lists, vals, field = pl.pallas_call(
        functools.partial(bin_kernel, z),
        out_shape=[
            pltpu.SMEM((z.list_len,), jnp.int32),
            pltpu.VMEM(tile_val.shape, BF16),
            z.block_vmem(z.nb, BF16),
        ],
        in_specs=[SMEM_SPEC] + [ANY_SPEC] * 6,
        out_specs=[SMEM_SPEC, VMEM_SPEC, VMEM_SPEC],
        scratch_shapes=[
            pltpu.SMEM(hub_ids.shape, jnp.int32),
            pltpu.SMEM(send_ids.shape, jnp.int32),
            pltpu.SMEM(tile_row.shape, jnp.int32),
            pltpu.SMEM(tile_col.shape, jnp.int32),
            pltpu.SMEM((z.nb + z.n_hub * z.hub + z.n_grp * z.tail,), jnp.int32),
            pltpu.SMEM((z.nb,), jnp.int32),
            pltpu.SMEM((4,), jnp.int32),
            pltpu.SemaphoreType.DMA((4,)),
            pltpu.SemaphoreType.DMA((2,)),
        ],
        compiler_params=PARAMS,
        cost_estimate=cost(z, 0, 2 * (2 * z.slots * z.blk * z.blk + z.field_bytes)),
        name="binning",
    )(tile_count, hub_ids, send_ids, hbm(tile_row), hbm(tile_col), hbm(tile_val), hbm(field0))

    acc_shape = z.block_vmem(z.nb + 1, F32)
    vals, field = vmem(vals), vmem(field)
    lists = pltpu.with_memory_space_constraint(lists, pltpu.SMEM)
    acc = pl.pallas_call(
        functools.partial(start_kernel, z),
        out_shape=acc_shape,
        in_specs=[SMEM_SPEC, VMEM_SPEC, VMEM_SPEC],
        out_specs=VMEM_SPEC,
        compiler_params=PARAMS,
        cost_estimate=cost(z, z.slots // 2, 3 * z.field_bytes),
        name="start",
    )(lists, vals, field)

    fields = [field]
    for step in range(ORDER):
        if step > 0:
            acc, rem, hub, *tails = pl.pallas_call(
                functools.partial(edge_kernel, z, late_parts, step),
                out_shape=[acc_shape, z.block_vmem(z.rem - z.rem_first, BF16)] + sent_shapes,
                in_specs=[SMEM_SPEC] + [VMEM_SPEC] * (3 + len(late_parts)),
                out_specs=[VMEM_SPEC] * (2 + len(sent_shapes)),
                input_output_aliases={3: 0},
                compiler_params=PARAMS,
                cost_estimate=cost(z, z.slots // 16, 2 * z.rem * z.blk * z.emb),
                name="edge",
            )(lists, vals, fields[max(step - 2, 0)], vmem(acc), *map(vmem, late))
            got, arrays, parts = first_stage(z, hub, tails)
            acc, new = pl.pallas_call(
                functools.partial(finish_kernel, z, step),
                out_shape=[acc_shape, z.block_vmem(z.nb, BF16)],
                in_specs=[SMEM_SPEC] + [VMEM_SPEC] * (3 + step),
                out_specs=[VMEM_SPEC] * 2,
                input_output_aliases={3 + step: 0},
                compiler_params=PARAMS,
                cost_estimate=cost(z, z.slots // 4, 5 * z.field_bytes),
                name="finish",
            )(lists, vals, vmem(rem), *fields, vmem(acc))
            fields.append(vmem(new))
        if step == 0:
            got, vals = lax.optimization_barrier((got, vals))
            vals = vmem(vals)
        else:
            got, acc = lax.optimization_barrier((got, acc))
        late, late_parts = second_stage(z, got)
        acc = pl.pallas_call(
            functools.partial(local_kernel, z, parts, step),
            out_shape=acc_shape,
            in_specs=[SMEM_SPEC] + [VMEM_SPEC] * (3 + len(parts)),
            out_specs=VMEM_SPEC,
            input_output_aliases={3: 0},
            scratch_shapes=[pltpu.VMEM((z.rem_first, z.blk, z.emb), BF16)],
            compiler_params=PARAMS,
            cost_estimate=cost(z, z.slots // 2, 0),
            name="local",
        )(lists, vals, fields[-1], vmem(acc), *map(vmem, arrays))

    _, out = pl.pallas_call(
        functools.partial(last_kernel, z, late_parts),
        out_shape=[acc_shape, z.block(z.nb, F32)],
        in_specs=[SMEM_SPEC] + [VMEM_SPEC] * (2 + len(late_parts)),
        out_specs=[VMEM_SPEC, ANY_SPEC],
        input_output_aliases={2: 0},
        scratch_shapes=[
            pltpu.VMEM((z.rem - z.rem_first, z.blk, z.emb), BF16),
            pltpu.SemaphoreType.DMA(()),
        ],
        compiler_params=PARAMS,
        name="last",
    )(lists, vals, vmem(acc), *map(vmem, late))
    return out.reshape(embed.shape[0], z.emb)


def solution(mesh):
    return jax.shard_map(
        functools.partial(shards, dict(mesh.shape)),
        mesh=mesh,
        in_specs=(
            P(("grp", "hub"), None),
            P(("grp", "hub"), None),
            P(("grp", "hub"), None, None),
            P(("grp", "hub"), None),
            P(("grp", "hub"), None),
            P(("grp", "hub"), None, None),
            P(("grp", "hub")),
        ),
        out_specs=P(("grp", "hub"), None),
        check_vma=False,
    )
```
